256 devices in a mesh: dom: 64 (over z, y_hi, x), orb: 4 (over y_lo, core).
Axes of the slice: x: 4, y: 4 (y_hi: 2, y_lo: 2; y = y_hi * 2 + y_lo), z: 8, core: 2. Of those that a mesh axis runs over, the one named last changes fastest.
Arguments:
- orbitals: float32 [16, 1024, 16, 128], P('orb', 'dom'), may hold values from -12 to 12, as said below
- local_potential: float32 [1024, 16, 128], P('dom'), may hold values from -3 to 1
- sphere_index: int32 [1024, 128], P('dom'), may hold values from -1 to 32767, as said below
- projector: float32 [1024, 4, 128], P('dom'), may hold values from -1 to 1
- species: int32 [1024], P('dom'), may hold values from 0 to 2
- atom_count: int32 [64], P('dom'), may hold values from 1 to 16, as said below
- channel_energy: float32 [3, 4], replicated, may hold values from 0.5 to 4
Outputs:
- filtered: float32 [16, 1024, 16, 128], P('orb', 'dom')
- gram: float32 [16, 16], replicated
The draws below stay inside these ranges and needn't reach their ends.
Inputs may be any that keep to these rules, and one draw needn't show every extreme that they name: `orbitals`: float entries; no further structure is promised. `sphere_index`: row a lists distinct cells of the slab of slot a, as flat indices (x * 16 + y) * 128 + z with x counted within the slab, followed by -1 entries as padding; a row holds 64 to 128 cells. `atom_count`: at most 16 live atoms on a slab; some slab holds exactly 16.
All inputs are finite; a program needn't handle non-finite values.
Results may differ from the reference program's by a relative error of at most 0.00011.
Values sent between devices are 32-bit elements; how exact they have to be, the bound alone decides.
No kernel may reach another device: no remote copies, remote signals or barrier semaphores. Data moves between devices by JAX's collectives and lax.ppermute only.
A program may use at most 128 MiB of HBM per device.

```python
import math
import jax
import jax.numpy as jnp
from jax import lax

CX = 16
CY = 16
CZ = 128
MAXA = 16
NORB = 16
NPROJ = 4
NSPEC = 3
NPTS = 128
RADIUS = 6
DOMAINS = 64
NX = 1024
ATOMS = 1024


def draw_orbitals(key, part):
    key = jax.random.fold_in(key, 11)
    key_own, key_common = jax.random.split(key, 2)
    own = jnp.clip(jax.random.normal(key_own, (NORB, NX, CY, CZ), jnp.float32), -4.0, 4.0)
    common = jnp.clip(jax.random.normal(key_common, (1, NX, CY, CZ), jnp.float32), -4.0, 4.0)
    rising = 3.0
    layers = jnp.arange(NX, dtype=jnp.float32) / (NX - 1)
    amplitude = jnp.power(rising, 0.5 * layers).reshape(1, NX, 1, 1)
    return (own + 0.6 * common) * amplitude


def draw_sphere_index(key, part):
    key = jax.random.fold_in(key, 5)
    key_x, key_y, key_z, key_used = jax.random.split(key, 4)
    slot_ids = jnp.arange(ATOMS, dtype=jnp.int32)[:, None]
    start_x = jax.random.randint(key_x, (ATOMS, 1), 0, CX - 7)
    centre_y = jax.random.randint(key_y, (ATOMS, 1), 0, CY)
    centre_z = jax.random.randint(key_z, (ATOMS, 1), 0, CZ)
    used_points = NPTS // 2 + jax.random.randint(key_used, (ATOMS, 1), 0, NPTS // 2 + 1)
    start_x = jnp.where(slot_ids == 0, CX - 8, start_x)
    centre_y = jnp.where(slot_ids == 0, CY - 2, centre_y)
    centre_z = jnp.where(slot_ids == 0, CZ - 2, centre_z)
    used_points = jnp.where(slot_ids == 0, NPTS, jnp.where(slot_ids == 1, NPTS // 2, used_points))
    points = jnp.arange(NPTS, dtype=jnp.int32)[None, :]
    cell_x = start_x + points // 16
    cell_y = (centre_y + points // 4 % 4 - 2) % CY
    cell_z = (centre_z + points % 4 - 2) % CZ
    flat_cells = (cell_x * CY + cell_y) * CZ + cell_z
    return jnp.where(points < used_points, flat_cells, -1).astype(jnp.int32)


def draw_atom_count(key, part):
    key = jax.random.fold_in(key, 7)
    key_count, key_busy = jax.random.split(key)
    rolled = jax.random.randint(key_count, (DOMAINS,), 0, MAXA + 1)
    counts = 1 + rolled * rolled // (MAXA + 1)
    busiest = jax.random.randint(key_busy, (), 0, DOMAINS)
    counts = jnp.where(jnp.arange(DOMAINS, dtype=jnp.int32) == busiest, MAXA, counts)
    return counts.astype(jnp.int32)


def touch_ends(entries, stream_key, low, high):
    index_at = [jax.random.randint(jax.random.fold_in(stream_key, axis), (), 0, length) for axis, length in enumerate(entries.shape)]
    main_axis = entries.shape.index(max(entries.shape))
    next_to = index_at[:main_axis] + [(index_at[main_axis] + 1) % entries.shape[main_axis]] + index_at[main_axis + 1:]
    return entries.at[tuple(index_at)].set(low).at[tuple(next_to)].set(high)


def steps_of(own_key, shape, cuts, smallest, largest):
    loudness, own = 1.0, jax.random.fold_in(own_key, 6)
    for axis_at, shards_of in cuts:
        heights = jnp.exp(jax.random.uniform(jax.random.fold_in(own, axis_at), (shards_of,), jnp.float32, smallest / len(cuts), largest / len(cuts)))
        loudness = loudness * jnp.repeat(heights, shape[axis_at] // shards_of).reshape([-1 if axis == axis_at else 1 for axis in range(len(shape))])
    return loudness


def gaussian(key, dims, scale, reach, cuts=(), held_as=jnp.bfloat16):
    array = scale * jax.random.normal(key, dims, jnp.float32)
    if cuts:
        array = array * steps_of(key, dims, cuts, -0.22, 0.18)
    return jnp.clip(array, -reach, reach).astype(held_as)


def setup_inputs(seed: int = 0) -> dict:
    splits = jax.random.split(jax.random.key(seed), 8)
    return {
        "orbitals": draw_orbitals(jax.random.fold_in(splits[7], 71), 0),
        "local_potential": jnp.clip(-3.0 + 4.0 * jax.random.uniform(splits[1], (NX, CY, CZ), jnp.float32) ** steps_of(splits[1], (NX, CY, CZ), ((0, 64),), -0.2, 0.2), -3.0, 1.0),
        "sphere_index": draw_sphere_index(jax.random.fold_in(splits[7], 71), 0),
        "projector": gaussian(splits[3], (ATOMS, NPROJ, NPTS), 32 ** -0.5, 1.0, ((0, 64),), jnp.float32),
        "species": touch_ends(jax.random.randint(splits[4], (ATOMS,), 0, NSPEC), jax.random.fold_in(splits[4], 1), 0, NSPEC - 1).astype(jnp.int32),
        "atom_count": draw_atom_count(jax.random.fold_in(splits[7], 71), 0),
        "channel_energy": jnp.clip(jnp.exp(jax.random.uniform(splits[6], (NSPEC, NPROJ), jnp.float32, math.log(0.5), math.log(4.0))), 0.5, 4.0),
    }


STENCIL = (-5369.0 / 1800.0, 12.0 / 7.0, -15.0 / 56.0, 10.0 / 189.0, -1.0 / 112.0, 2.0 / 1925.0, -1.0 / 16632.0)
LOWER_EDGE = 2.0
UPPER_EDGE = 17.0
HIGHEST = lax.Precision.HIGHEST


def nonlocal_part(orb_block, global_cells, in_sphere, projector, strength):
    orb_count = orb_block.shape[0]
    flat_block = orb_block.reshape(orb_count, -1)
    picked = jnp.take(flat_block, global_cells.reshape(-1), axis=1).reshape(orb_count, ATOMS, NPTS)
    picked = jnp.where(in_sphere[None], picked, 0.0)
    coefficient = jnp.einsum("apk,oak->oap", projector, picked, precision=HIGHEST)
    scaled = coefficient * strength[None]
    spread = jnp.einsum("apk,oap->oak", projector, scaled, precision=HIGHEST)
    spread = jnp.where(in_sphere[None], spread, 0.0)
    accumulated = jnp.zeros_like(flat_block).at[:, global_cells.reshape(-1)].add(spread.reshape(orb_count, -1))
    return accumulated.reshape(orb_block.shape)


def apply_operator(orb_block, potential, global_cells, in_sphere, projector, strength):
    lap_total = 3.0 * STENCIL[0] * orb_block
    for offset in range(1, RADIUS + 1):
        neighbours = jnp.roll(orb_block, offset, 1) + jnp.roll(orb_block, -offset, 1)
        neighbours = neighbours + jnp.roll(orb_block, offset, 2) + jnp.roll(orb_block, -offset, 2)
        neighbours = neighbours + jnp.roll(orb_block, offset, 3) + jnp.roll(orb_block, -offset, 3)
        lap_total = lap_total + STENCIL[offset] * neighbours
    return -0.5 * lap_total + potential[None] * orb_block + nonlocal_part(orb_block, global_cells, in_sphere, projector, strength)


def reference(orbitals, local_potential, sphere_index, projector, species, atom_count, channel_energy):
    slots = jnp.arange(ATOMS, dtype=jnp.int32)
    home_slab = slots // MAXA
    onehot = (species[:, None] == jnp.arange(NSPEC, dtype=jnp.int32)[None, :]).astype(jnp.float32)
    is_live = (slots % MAXA) < atom_count[home_slab]
    strength = jnp.where(is_live[:, None], jnp.dot(onehot, channel_energy, precision=HIGHEST), 0.0)
    in_sphere = sphere_index >= 0
    global_cells = jnp.where(in_sphere, sphere_index + home_slab[:, None] * (CX * CY * CZ), 0).astype(jnp.int32)
    mid_point = 0.5 * (UPPER_EDGE + LOWER_EDGE)
    half_width = 0.5 * (UPPER_EDGE - LOWER_EDGE)
    step_one = (apply_operator(orbitals, local_potential, global_cells, in_sphere, projector, strength) - mid_point * orbitals) / half_width
    filtered = 2.0 * (apply_operator(step_one, local_potential, global_cells, in_sphere, projector, strength) - mid_point * step_one) / half_width - orbitals
    flat_rows = filtered.reshape(NORB, -1)
    gram = lax.dot_general(flat_rows, flat_rows, (((1,), (1,)), ((), ())), precision=HIGHEST) / (NX * CY * CZ)
    return filtered, gram
```

```python
import functools

import jax
import jax.numpy as jnp
from jax import lax
from jax.experimental import pallas as pl
from jax.experimental.pallas import tpu as pltpu
from jax.sharding import PartitionSpec as P

RADIUS = 6
STENCIL = (
    -5369.0 / 1800.0,
    12.0 / 7.0,
    -15.0 / 56.0,
    10.0 / 189.0,
    -1.0 / 112.0,
    2.0 / 1925.0,
    -1.0 / 16632.0,
)
LOWER_EDGE = 2.0
UPPER_EDGE = 17.0
MID_POINT = 0.5 * (UPPER_EDGE + LOWER_EDGE)
HALF_WIDTH = 0.5 * (UPPER_EDGE - LOWER_EDGE)
VMEM = pltpu.VMEM
SMEM = pltpu.SMEM
NT = (((1,), (1,)), ((), ()))


def split(values):
    high = values.astype(jnp.bfloat16)
    return high, (values - high.astype(jnp.float32)).astype(jnp.bfloat16)


def nonlocal_rows(
    load_rows, orbs, index, projector, species, count, energy, parts, rowhot, zhot, picked, spread
):
    rows, lanes = 256, 128
    atoms, channels = projector.shape[0], projector.shape[1]
    for o in range(orbs):
        high, low = split(load_rows(o).T)
        parts[0, o * lanes : (o + 1) * lanes, :] = high
        parts[1, o * lanes : (o + 1) * lanes, :] = low
    cells = index[...]
    row_of = cells >> 7
    lane_of = cells & 127
    row_iota = lax.broadcasted_iota(jnp.int32, (rows, lanes), 0)
    lane_iota = lax.broadcasted_iota(jnp.int32, (lanes, lanes), 0)
    for a in range(atoms):
        at = slice(a * lanes, (a + 1) * lanes)
        rowhot[:, at] = jnp.where(row_iota == row_of[a : a + 1], 1.0, 0.0).astype(jnp.bfloat16)
    for a in range(0, atoms, 2):
        at = slice(a * lanes, (a + 2) * lanes)
        found = jnp.dot(parts[0], rowhot[:, at], preferred_element_type=jnp.float32)
        found = found + jnp.dot(parts[1], rowhot[:, at], preferred_element_type=jnp.float32)
        for b in range(2):
            hot = lane_iota == lane_of[a + b : a + b + 1]
            zhot[:, (a + b) * lanes : (a + b + 1) * lanes] = jnp.where(hot, 1.0, 0.0).astype(
                jnp.bfloat16
            )
            for o in range(orbs):
                block = found[o * lanes : (o + 1) * lanes, b * lanes : (b + 1) * lanes]
                picked[o, a + b : a + b + 1, :] = jnp.sum(
                    jnp.where(hot, block, 0.0), axis=0, keepdims=True
                )
    slot = lax.broadcasted_iota(jnp.int32, (atoms, 1), 0)
    live = slot < count[0]
    inside = cells >= 0
    total = [jnp.zeros((atoms, lanes), jnp.float32) for _ in range(orbs)]
    for p in range(channels):
        strength = jnp.zeros((atoms, 1), jnp.float32)
        for a in range(atoms):
            strength = jnp.where(slot == a, energy[species[a], p], strength)
        strength = jnp.where(live, strength, 0.0)
        shape = projector[:, p, :]
        for o in range(orbs):
            coefficient = jnp.sum(shape * picked[o], axis=1, keepdims=True)
            total[o] = total[o] + shape * (coefficient * strength)
    for o in range(orbs):
        high, low = split(jnp.where(inside, total[o], 0.0))
        for a in range(atoms):
            at = slice(a * lanes, (a + 1) * lanes)
            hot = zhot[:, at]
            spread[0, o * lanes : (o + 1) * lanes, at] = hot * high[a : a + 1]
            spread[1, o * lanes : (o + 1) * lanes, at] = hot * low[a : a + 1]
    out = lax.dot_general(rowhot[...], spread[0], NT, preferred_element_type=jnp.float32)
    return out + lax.dot_general(rowhot[...], spread[1], NT, preferred_element_type=jnp.float32)


def local_layer(load, potential, i, layers):
    centre = load(i)
    total = (potential - (1.5 * STENCIL[0] + MID_POINT)) * centre
    for k in range(1, RADIUS + 1):
        near = pltpu.roll(centre, k, 0) + pltpu.roll(centre, centre.shape[0] - k, 0)
        near = near + pltpu.roll(centre, k, 1) + pltpu.roll(centre, centre.shape[1] - k, 1)
        if i - k >= 0:
            near = near + load(i - k)
        if i + k < layers:
            near = near + load(i + k)
        total = total - (0.5 * STENCIL[k]) * near
    return total


def first_kernel(
    species, count, energy, v, potential, index, projector, out, parts, rowhot, zhot, picked, spread
):
    orbs, layers = v.shape[0], v.shape[1]
    hat = nonlocal_rows(
        lambda o: v[o].reshape(256, 128),
        orbs,
        index,
        projector,
        species,
        count,
        energy,
        parts,
        rowhot,
        zhot,
        picked,
        spread,
    )
    for o in range(orbs):
        for i in range(layers):
            total = local_layer(lambda j: v[o, j], potential[i], i, layers)
            total = total + hat[i * 16 : (i + 1) * 16, o * 128 : (o + 1) * 128]
            out[o, i] = total * (1.0 / HALF_WIDTH)


def second_kernel(
    species,
    count,
    energy,
    v,
    potential,
    index,
    projector,
    low,
    middle,
    high,
    out,
    parts,
    rowhot,
    zhot,
    picked,
    spread,
    held,
):
    orbs, layers = v.shape[0], v.shape[1]
    held[:, :RADIUS] = low[...]
    held[:, RADIUS : layers - RADIUS] = middle[:, RADIUS : layers - RADIUS]
    held[:, layers - RADIUS :] = high[...]
    hat = nonlocal_rows(
        lambda o: held[o].reshape(256, 128),
        orbs,
        index,
        projector,
        species,
        count,
        energy,
        parts,
        rowhot,
        zhot,
        picked,
        spread,
    )
    for o in range(orbs):
        for i in range(layers):
            total = local_layer(lambda j: held[o, j], potential[i], i, layers)
            total = total + hat[i * 16 : (i + 1) * 16, o * 128 : (o + 1) * 128]
            out[o, i] = total * (2.0 / HALF_WIDTH) - v[o, i]


def from_below(below, o, i):
    total = STENCIL[i + 1] * below[o, RADIUS - 1]
    for k in range(i + 2, RADIUS + 1):
        total = total + STENCIL[k] * below[o, RADIUS + i - k]
    return total


def from_above(above, o, j):
    total = STENCIL[j + 1] * above[o, 0]
    for k in range(j + 2, RADIUS + 1):
        total = total + STENCIL[k] * above[o, k - j - 1]
    return total


def first_edges(part, below, above, low, high):
    orbs, layers = part.shape[0], part.shape[1]
    scale = -0.5 / HALF_WIDTH
    for o in range(orbs):
        for i in range(RADIUS):
            low[o, i] = part[o, i] + scale * from_below(below, o, i)
            high[o, RADIUS - 1 - i] = part[o, layers - 1 - i] + scale * from_above(above, o, i)


def second_edges(me, part, below, above, out, own, send_1, send_2, send_3):
    orbs, layers = part.shape[0], part.shape[1]
    scale = -1.0 / HALF_WIDTH
    out[:, RADIUS : layers - RADIUS] = part[:, RADIUS : layers - RADIUS]
    for o in range(orbs):
        for i in range(RADIUS):
            out[o, i] = part[o, i] + scale * from_below(below, o, i)
            out[o, layers - 1 - i] = part[o, layers - 1 - i] + scale * from_above(above, o, i)
    depth = own.shape[1]
    for k, chunk in enumerate((own, send_1, send_2, send_3)):
        first = pl.multiple_of((me[0] ^ k) * depth, depth)
        for o in range(orbs):
            chunk[o] = out[o, pl.ds(first, depth)]


def gram_kernel(me, own, got_1, got_2, got_3, out, rows):
    orbs, depth = own.shape[0], own.shape[1]
    for k, chunk in enumerate((own, got_1, got_2, got_3)):
        first = (me[0] ^ k) * orbs
        for o in range(orbs):
            for x in range(depth):
                rows[x, first + o] = chunk[o, x]
    total = jnp.zeros((256, 256), jnp.float32)
    for x in range(depth):
        high, low = split(rows[x].reshape(256, 128))
        left = jnp.concatenate([high, high, low], axis=1)
        right = jnp.concatenate([high, low, high], axis=1)
        total = total + lax.dot_general(left, right, NT, preferred_element_type=jnp.float32)
    same = (lax.broadcasted_iota(jnp.int32, (256, 256), 0) & 15) == (
        lax.broadcasted_iota(jnp.int32, (256, 256), 1) & 15
    )
    total = jnp.where(same, total, 0.0)
    total = jnp.sum(total.reshape(16, 16, 256), axis=1)
    lane = lax.broadcasted_iota(jnp.int32, (256, 128), 1)
    place = (lane & 15) == (lax.broadcasted_iota(jnp.int32, (256, 128), 0) >> 4)
    place = jnp.where(place, 1.0, 0.0)
    spread = jnp.dot(
        total, place, precision=lax.Precision.HIGHEST, preferred_element_type=jnp.float32
    )
    keep = (lax.broadcasted_iota(jnp.int32, (16, 128), 1) >> 4) == (
        lax.broadcasted_iota(jnp.int32, (16, 128), 0) & 7
    )
    spread = jnp.where(keep, spread, 0.0)
    packed = jnp.sum(spread.reshape(2, 8, 128), axis=1)
    out[...] = jnp.broadcast_to(packed[None], out.shape)


def final_kernel(cells, terms, out):
    packed = jnp.sum(terms[...], axis=0)
    row = lax.broadcasted_iota(jnp.int32, (16, 128), 0)
    lane = lax.broadcasted_iota(jnp.int32, (16, 128), 1)
    spread = jnp.where(row < 8, packed[0:1], packed[1:2])
    spread = jnp.where((lane >> 4) == (row & 7), spread, 0.0)
    place = (lax.broadcasted_iota(jnp.int32, (128, 16), 0) & 15) == lax.broadcasted_iota(
        jnp.int32, (128, 16), 1
    )
    place = jnp.where(place, 1.0, 0.0)
    total = jnp.dot(
        spread, place, precision=lax.Precision.HIGHEST, preferred_element_type=jnp.float32
    )
    out[...] = total * (1.0 / cells)


def call(kernel, outs, in_specs, scratch=(), flops=10_000_000, limit=48 * 2**20):
    return pl.pallas_call(
        kernel,
        out_shape=outs,
        in_specs=in_specs,
        out_specs=jax.tree.map(lambda _: pl.BlockSpec(memory_space=VMEM), outs),
        scratch_shapes=list(scratch),
        compiler_params=pltpu.CompilerParams(vmem_limit_bytes=limit),
        cost_estimate=pl.CostEstimate(flops=flops, bytes_accessed=2**21, transcendentals=0),
    )


def on_device(
    orbitals, local_potential, sphere_index, projector, species, atom_count, channel_energy
):
    f32 = jnp.float32
    in_vmem = pl.BlockSpec(memory_space=VMEM)
    in_smem = pl.BlockSpec(memory_space=SMEM)
    orbs, layers, wide, deep = orbitals.shape
    doms, orb_devices = lax.axis_size("dom"), lax.axis_size("orb")
    up = [(i, (i + 1) % doms) for i in range(doms)]
    down = [((i + 1) % doms, i) for i in range(doms)]
    me = lax.axis_index("orb").astype(jnp.int32).reshape(1)
    edge = jax.ShapeDtypeStruct((orbs, RADIUS, wide, deep), f32)
    block = jax.ShapeDtypeStruct(orbitals.shape, f32)
    points = sphere_index.shape[0] * sphere_index.shape[1]
    scratch = [
        pltpu.VMEM((2, orbs * deep, layers * wide), jnp.bfloat16),
        pltpu.VMEM((layers * wide, points), jnp.bfloat16),
        pltpu.VMEM((deep, points), jnp.bfloat16),
        pltpu.VMEM((orbs,) + sphere_index.shape, f32),
        pltpu.VMEM((2, orbs * deep, points), jnp.bfloat16),
    ]
    scalars = (species, atom_count, channel_energy)
    fields = (orbitals, local_potential, sphere_index, projector)

    below = lax.ppermute(orbitals[:, layers - RADIUS :], "dom", up)
    above = lax.ppermute(orbitals[:, :RADIUS], "dom", down)
    part = call(
        first_kernel, block, [in_smem] * 3 + [in_vmem] * 4, scratch, flops=3_000_000_000
    )(*scalars, *fields)
    low, high = call(first_edges, (edge, edge), [in_vmem] * 3)(part, below, above)

    below = lax.ppermute(high, "dom", up)
    above = lax.ppermute(low, "dom", down)
    part = call(
        second_kernel,
        block,
        [in_smem] * 3 + [in_vmem] * 7,
        scratch + [pltpu.VMEM(orbitals.shape, f32)],
        flops=3_000_000_000,
    )(*scalars, *fields, low, part, high)
    quarter = jax.ShapeDtypeStruct((orbs, layers // orb_devices, wide, deep), f32)
    filtered, own, *sends = call(
        second_edges, (block,) + (quarter,) * 4, [in_smem] + [in_vmem] * 3
    )(me, part, below, above)

    got = [
        lax.ppermute(sends[k - 1], "orb", [(i, i ^ k) for i in range(orb_devices)])
        for k in (1, 2, 3)
    ]
    everyone = doms * orb_devices
    terms = call(
        gram_kernel,
        jax.ShapeDtypeStruct((everyone, 2, 128), f32),
        [in_smem] + [in_vmem] * 4,
        [pltpu.VMEM((layers // orb_devices, orbs * orb_devices, wide, deep), f32)],
    )(me, own, *got)
    terms = lax.all_to_all(terms, ("dom", "orb"), 0, 0)
    gram = call(
        functools.partial(final_kernel, float(layers * wide * deep * doms)),
        jax.ShapeDtypeStruct((16, 16), f32),
        [in_vmem],
    )(terms)
    return filtered, gram


def solution(mesh):
    placed = (
        P("orb", "dom", None, None),
        P("dom", None, None),
        P("dom", None),
        P("dom", None, None),
        P("dom"),
        P("dom"),
        P(),
    )
    return jax.shard_map(
        on_device,
        mesh=mesh,
        in_specs=placed,
        out_specs=(P("orb", "dom", None, None), P()),
        check_vma=False,
    )
```

```python
import functools

import jax
import jax.numpy as jnp
from jax import lax
from jax.experimental import pallas as pl
from jax.experimental.pallas import tpu as pltpu
from jax.sharding import PartitionSpec as P

RADIUS = 6
STENCIL = (
    -5369.0 / 1800.0,
    12.0 / 7.0,
    -15.0 / 56.0,
    10.0 / 189.0,
    -1.0 / 112.0,
    2.0 / 1925.0,
    -1.0 / 16632.0,
)
LOWER_EDGE = 2.0
UPPER_EDGE = 17.0
MID_POINT = 0.5 * (UPPER_EDGE + LOWER_EDGE)
HALF_WIDTH = 0.5 * (UPPER_EDGE - LOWER_EDGE)
VMEM = pltpu.VMEM
NT = (((1,), (1,)), ((), ()))


def split(values):
    high = values.astype(jnp.bfloat16)
    return high, (values - high.astype(jnp.float32)).astype(jnp.bfloat16)


def place(condition):
    return jnp.where(condition, 1.0, 0.0).astype(jnp.bfloat16)


def mark_cells(index, rowhot, zhot):
    cells = index[...]
    row_of = cells >> 7
    lane_of = cells & 127
    row_iota = lax.broadcasted_iota(jnp.int32, (256, 128), 0)
    for a in range(cells.shape[0]):
        at = slice(a * 128, (a + 1) * 128)
        rowhot[:, at] = place(row_iota == row_of[a : a + 1])
        zhot[:, at] = place(row_iota[:128] == lane_of[a : a + 1])


def nonlocal_rows(load_rows, orbs, index, projector, strength, parts, rowhot, zhot, picked, spread):
    lanes = 128
    atoms, channels = projector.shape[0], projector.shape[1]
    for o in range(orbs):
        high, low = split(load_rows(o).T)
        parts[0, o * lanes : (o + 1) * lanes, :] = high
        parts[1, o * lanes : (o + 1) * lanes, :] = low
    cells = index[...]
    lane_of = cells & 127
    lane_iota = lax.broadcasted_iota(jnp.int32, (lanes, lanes), 0)
    for a in range(0, atoms, 2):
        at = slice(a * lanes, (a + 2) * lanes)
        found = jnp.dot(parts[0], rowhot[:, at], preferred_element_type=jnp.float32)
        found = found + jnp.dot(parts[1], rowhot[:, at], preferred_element_type=jnp.float32)
        for b in range(2):
            hot = lane_iota == lane_of[a + b : a + b + 1]
            for o in range(orbs):
                block = found[o * lanes : (o + 1) * lanes, b * lanes : (b + 1) * lanes]
                picked[o, a + b : a + b + 1, :] = jnp.sum(
                    jnp.where(hot, block, 0.0), axis=0, keepdims=True
                )
    inside = cells >= 0
    total = [jnp.zeros((atoms, lanes), jnp.float32) for _ in range(orbs)]
    for p in range(channels):
        shape = projector[:, p, :]
        for o in range(orbs):
            coefficient = jnp.sum(shape * picked[o], axis=1, keepdims=True)
            total[o] = total[o] + shape * (coefficient * strength[p])
    for o in range(orbs):
        high, low = split(jnp.where(inside, total[o], 0.0))
        for a in range(atoms):
            at = slice(a * lanes, (a + 1) * lanes)
            hot = zhot[:, at]
            spread[0, o * lanes : (o + 1) * lanes, at] = hot * high[a : a + 1]
            spread[1, o * lanes : (o + 1) * lanes, at] = hot * low[a : a + 1]
    out = lax.dot_general(rowhot[...], spread[0], NT, preferred_element_type=jnp.float32)
    return out + lax.dot_general(rowhot[...], spread[1], NT, preferred_element_type=jnp.float32)


def local_layer(load, potential, i, layers):
    centre = load(i)
    total = (potential - (1.5 * STENCIL[0] + MID_POINT)) * centre
    for k in range(1, RADIUS + 1):
        near = pltpu.roll(centre, k, 0) + pltpu.roll(centre, centre.shape[0] - k, 0)
        near = near + pltpu.roll(centre, k, 1) + pltpu.roll(centre, centre.shape[1] - k, 1)
        if i - k >= 0:
            near = near + load(i - k)
        if i + k < layers:
            near = near + load(i + k)
        total = total - (0.5 * STENCIL[k]) * near
    return total


def first_kernel(
    species,
    count,
    energy,
    v,
    potential,
    index,
    projector,
    out,
    rowhot,
    zhot,
    strength,
    parts,
    picked,
    spread,
):
    orbs, layers = v.shape[0], v.shape[1]
    slot_strengths(species, count, energy, strength)
    mark_cells(index, rowhot, zhot)
    hat = nonlocal_rows(
        lambda o: v[o].reshape(256, 128),
        orbs,
        index,
        projector,
        strength,
        parts,
        rowhot,
        zhot,
        picked,
        spread,
    )
    for o in range(orbs):
        for i in range(layers):
            total = local_layer(lambda j: v[o, j], potential[i], i, layers)
            total = total + hat[i * 16 : (i + 1) * 16, o * 128 : (o + 1) * 128]
            out[o, i] = total * (1.0 / HALF_WIDTH)


def second_kernel(
    v,
    potential,
    index,
    projector,
    strength,
    rowhot,
    zhot,
    near,
    far,
    middle,
    out,
    parts,
    picked,
    spread,
    held,
):
    orbs, layers = v.shape[0], v.shape[1]
    first, last = far_near_starts(layers)
    held[:, pl.ds(first, RADIUS)] = far[...]
    held[:, pl.ds(last, RADIUS)] = near[...]
    held[:, RADIUS : layers - RADIUS] = middle[:, RADIUS : layers - RADIUS]
    hat = nonlocal_rows(
        lambda o: held[o].reshape(256, 128),
        orbs,
        index,
        projector,
        strength,
        parts,
        rowhot,
        zhot,
        picked,
        spread,
    )
    for o in range(orbs):
        for i in range(layers):
            total = local_layer(lambda j: held[o, j], potential[i], i, layers)
            total = total + hat[i * 16 : (i + 1) * 16, o * 128 : (o + 1) * 128]
            out[o, i] = total * (2.0 / HALF_WIDTH) - v[o, i]


def from_below(below, o, i):
    total = STENCIL[i + 1] * below[o, RADIUS - 1]
    for k in range(i + 2, RADIUS + 1):
        total = total + STENCIL[k] * below[o, RADIUS + i - k]
    return total


def from_above(above, o, j):
    total = STENCIL[j + 1] * above[o, 0]
    for k in range(j + 2, RADIUS + 1):
        total = total + STENCIL[k] * above[o, k - j - 1]
    return total


def far_near_starts(layers):
    odd = lax.axis_index("dom") & 1
    first = odd * (layers - RADIUS)
    return first, layers - RADIUS - first


def by_parity(body, far, near):
    odd = lax.axis_index("dom") & 1

    @pl.when(odd == 0)
    def _():
        body(far, near)

    @pl.when(odd == 1)
    def _():
        body(near, far)


def order_edges(low, high, far, near):
    def body(far_edge, near_edge):
        far[...] = far_edge[...]
        near[...] = near_edge[...]

    by_parity(body, low, high)


def slot_strengths(species, count, energy, strength):
    channels, atoms = strength.shape[0], strength.shape[1]
    slot = lax.broadcasted_iota(jnp.int32, (atoms, 128), 0)
    live = slot < count[0]
    for p in range(channels):
        total = jnp.zeros((atoms, 128), jnp.float32)
        for a in range(atoms):
            total = jnp.where(slot == a, energy[species[a], p], total)
        strength[p] = jnp.where(live, total, 0.0)


def first_edge(far_side, part, got, edge):
    orbs, layers = part.shape[0], part.shape[1]
    scale = -0.5 / HALF_WIDTH
    odd = lax.axis_index("dom") & 1

    @pl.when(odd == (0 if far_side else 1))
    def _():
        for o in range(orbs):
            for i in range(RADIUS):
                edge[o, i] = part[o, i] + scale * from_below(got, o, i)

    @pl.when(odd == (1 if far_side else 0))
    def _():
        for o in range(orbs):
            for i in range(RADIUS):
                at = layers - 1 - i
                edge[o, RADIUS - 1 - i] = part[o, at] + scale * from_above(got, o, i)


def deal(block, chunks):
    me = lax.axis_index("orb")
    depth = chunks[0].shape[1]
    for k, chunk in enumerate(chunks):
        first = (me ^ k) * depth
        for o in range(block.shape[0]):
            chunk[o] = block[o, pl.ds(first, depth)]


def second_near(part, got, block, *chunks):
    orbs, layers = part.shape[0], part.shape[1]
    scale = -1.0 / HALF_WIDTH
    odd = lax.axis_index("dom") & 1

    @pl.when(odd == 0)
    def _():
        for o in range(orbs):
            for i in range(RADIUS, layers):
                rows = part[o, i]
                if i >= layers - RADIUS:
                    rows = rows + scale * from_above(got, o, layers - 1 - i)
                block[o, 2 * (i - RADIUS) : 2 * (i - RADIUS) + 2] = rows.reshape(2, 8, 128)

    @pl.when(odd == 1)
    def _():
        for o in range(orbs):
            for i in range(layers - RADIUS):
                rows = part[o, i]
                if i < RADIUS:
                    rows = rows + scale * from_below(got, o, i)
                block[o, 2 * i : 2 * i + 2] = rows.reshape(2, 8, 128)

    deal(block, chunks)


def second_far(part, got, block, *chunks):
    orbs, layers = part.shape[0], part.shape[1]
    scale = -1.0 / HALF_WIDTH
    odd = lax.axis_index("dom") & 1

    @pl.when(odd == 0)
    def _():
        for o in range(orbs):
            for i in range(RADIUS):
                rows = part[o, i] + scale * from_below(got, o, i)
                block[o, 2 * i : 2 * i + 2] = rows.reshape(2, 8, 128)

    @pl.when(odd == 1)
    def _():
        for o in range(orbs):
            for i in range(RADIUS):
                rows = part[o, layers - 1 - i] + scale * from_above(got, o, i)
                at = 2 * (RADIUS - 1 - i)
                block[o, at : at + 2] = rows.reshape(2, 8, 128)

    deal(block, chunks)


def split_3(values):
    high = values.astype(jnp.bfloat16)
    rest = values - high.astype(jnp.float32)
    middle = rest.astype(jnp.bfloat16)
    low = (rest - middle.astype(jnp.float32)).astype(jnp.bfloat16)
    return jnp.concatenate([high, middle, low], axis=0)


def lane_block(lane):
    block = lane >> 4
    first = jnp.where(block < 3, 0, jnp.where(block < 5, 1, 2))
    second = jnp.where(block < 3, block + 1, jnp.where(block < 5, block - 1, 3))
    return block, 4 * first + ((lane >> 2) & 3), 4 * second + (lane & 3)


def row_products(loads, rows, left_rows, right_rows):
    total = None
    for load in loads:
        high, low = split(load().reshape(rows, 128))
        left = jnp.concatenate([high, high, low], axis=1)[left_rows]
        right = jnp.concatenate([high, low, high], axis=1)[right_rows]
        term = lax.dot_general(left, right, NT, preferred_element_type=jnp.float32)
        total = term if total is None else total + term
    row = lax.broadcasted_iota(jnp.int32, total.shape, 0)
    column = lax.broadcasted_iota(jnp.int32, total.shape, 1)
    total = jnp.where((row & 7) == (column & 7), total, 0.0)
    return jnp.sum(total.reshape(total.shape[0] // 8, 8, total.shape[1]), axis=1)


def pack(sums, column_orbital, row_orbital):
    count, columns = sums.shape
    lane = lax.broadcasted_iota(jnp.int32, (columns, 128), 1)
    orbital = lax.broadcasted_iota(jnp.int32, (columns, 128), 0) >> 3
    wide = jnp.dot(
        split_3(sums),
        place(orbital == column_orbital(lane)),
        preferred_element_type=jnp.float32,
    )
    wide = wide[:count] + wide[count : 2 * count] + wide[2 * count :]
    lane = lax.broadcasted_iota(jnp.int32, (count, 128), 1)
    orbital = lax.broadcasted_iota(jnp.int32, (count, 128), 0)
    return jnp.sum(jnp.where(orbital == row_orbital(lane), wide, 0.0), axis=0, keepdims=True)


def own_gram(early, near, far, out, own):
    orbs, layers = out.shape[0], out.shape[1]
    first, _ = far_near_starts(layers)
    rest = RADIUS - (first * RADIUS) // (layers - RADIUS)
    out[:, pl.ds(first, RADIUS)] = far[...].reshape(orbs, RADIUS, 16, 128)
    out[:, pl.ds(rest, layers - RADIUS)] = near[...].reshape(orbs, layers - RADIUS, 16, 128)
    everything = slice(None)
    loads = [lambda h=h: near[:, h] for h in range(near.shape[1])]
    loads += [lambda h=h: far[:, h] for h in range(far.shape[1])]
    sums = row_products(loads, 8 * orbs, everything, everything)
    sums = jnp.concatenate([sums, jnp.zeros_like(sums)], axis=0)
    lanes = pack(sums, lambda lane: lane & 3, lambda lane: (lane >> 2) & 3)
    lane = lax.broadcasted_iota(jnp.int32, (1, 128), 1)
    own[...] = early[...] + jnp.where((lane >= 96) & (lane < 112), lanes, 0.0)


def gram_lanes(chunks, rows):
    orbs, depth = chunks[0].shape[0], chunks[0].shape[1]
    me = lax.axis_index("orb")
    for k, chunk in enumerate(chunks):
        first = (me ^ k) * orbs
        for o in range(orbs):
            for h in range(depth):
                rows[h, first + o] = chunk[o, h]
    loads = [lambda h=h: rows[h] for h in range(depth)]
    sums = row_products(loads, 128, slice(0, 96), slice(32, 128))
    sums = jnp.concatenate([sums, jnp.zeros((4, 96), jnp.float32)], axis=0)
    lanes = pack(sums, lambda lane: lane_block(lane)[2] - 4, lambda lane: lane_block(lane)[1])
    lane = lax.broadcasted_iota(jnp.int32, (1, 128), 1)
    return jnp.where(lane < 96, lanes, 0.0)


def near_gram(got_2, got_3, got_1, own, out, rows):
    out[...] = gram_lanes((own, got_1, got_2, got_3), rows)


def far_gram(others, got_2, got_3, got_1, own, out, rows):
    lanes = gram_lanes((own, got_1, got_2, got_3), rows) + others[...]
    out[...] = jnp.broadcast_to(lanes[None], out.shape)


def final_kernel(cells, terms, out):
    orbs = 4
    sums = [terms[q] for q in range(orbs)]
    for d in range(1, terms.shape[0] // orbs):
        for q in range(orbs):
            sums[q] = sums[q] + terms[d * orbs + q]
    across = sums[0] + sums[1] + sums[2] + sums[3]
    row = lax.broadcasted_iota(jnp.int32, (16, 128), 0)
    lane = lax.broadcasted_iota(jnp.int32, (16, 128), 1)
    block, first, second = lane_block(lane)
    own = jnp.where(
        row < 8,
        jnp.where(row < 4, sums[0], sums[1]),
        jnp.where(row < 12, sums[2], sums[3]),
    )
    upper = jnp.where((block < 6) & (first == row), across, 0.0)
    lower = jnp.where((block < 6) & (second == row), across, 0.0)
    own = jnp.where((block == 6) & (((lane >> 2) & 3) == (row & 3)), own, 0.0)
    column = lax.broadcasted_iota(jnp.int32, (128, 16), 1)
    lane = lax.broadcasted_iota(jnp.int32, (128, 16), 0)
    block, first, second = lane_block(lane)

    def unpack(values, condition):
        parts = jnp.dot(split_3(values), place(condition), preferred_element_type=jnp.float32)
        return parts[:16] + parts[16:32] + parts[32:]

    total = unpack(upper, second == column) + unpack(lower, first == column)
    same = (lax.broadcasted_iota(jnp.int32, (16, 16), 0) >> 2) == (
        lax.broadcasted_iota(jnp.int32, (16, 16), 1) >> 2
    )
    total = total + jnp.where(same, unpack(own, (lane & 3) == (column & 3)), 0.0)
    out[...] = total * (1.0 / cells)


def call(kernel, outs, in_specs, scratch=(), flops=10_000_000, limit=48 * 2**20):
    return pl.pallas_call(
        kernel,
        out_shape=outs,
        in_specs=in_specs,
        out_specs=jax.tree.map(lambda _: pl.BlockSpec(memory_space=VMEM), outs),
        scratch_shapes=list(scratch),
        compiler_params=pltpu.CompilerParams(vmem_limit_bytes=limit),
        cost_estimate=pl.CostEstimate(flops=flops, bytes_accessed=2**21, transcendentals=0),
    )


def on_device(
    orbitals, local_potential, sphere_index, projector, species, atom_count, channel_energy
):
    f32 = jnp.float32
    in_vmem = pl.BlockSpec(memory_space=VMEM)
    orbs, layers, wide, deep = orbitals.shape
    doms, orb_devices = lax.axis_size("dom"), lax.axis_size("orb")
    far_pairs = [(i, (i - 1 if i % 2 == 0 else i + 1) % doms) for i in range(doms)]
    near_pairs = [(i, i ^ 1) for i in range(doms)]
    edge = jax.ShapeDtypeStruct((orbs, RADIUS, wide, deep), f32)
    block = jax.ShapeDtypeStruct(orbitals.shape, f32)
    atoms, points = sphere_index.shape
    in_smem = pl.BlockSpec(memory_space=pltpu.SMEM)
    scalars = (species, atom_count, channel_energy)
    fields = (orbitals, local_potential, sphere_index, projector)
    far, near = call(order_edges, (edge, edge), [in_vmem] * 2)(
        orbitals[:, :RADIUS], orbitals[:, layers - RADIUS :]
    )
    got_far = lax.ppermute(far, "dom", far_pairs)
    got_near = lax.ppermute(near, "dom", near_pairs)
    scratch = [
        pltpu.VMEM((2, orbs * deep, layers * wide), jnp.bfloat16),
        pltpu.VMEM((orbs,) + sphere_index.shape, f32),
        pltpu.VMEM((2, orbs * deep, atoms * points), jnp.bfloat16),
    ]
    part, rowhot, zhot, strength = call(
        first_kernel,
        (
            block,
            jax.ShapeDtypeStruct((layers * wide, atoms * points), jnp.bfloat16),
            jax.ShapeDtypeStruct((deep, atoms * points), jnp.bfloat16),
            jax.ShapeDtypeStruct((projector.shape[1], atoms, deep), f32),
        ),
        [in_smem] * 3 + [in_vmem] * 4,
        scratch,
        flops=3_000_000_000,
    )(*scalars, *fields)
    near = call(functools.partial(first_edge, False), edge, [in_vmem] * 2)(part, got_near)
    got_near = lax.ppermute(near, "dom", near_pairs)
    far = call(functools.partial(first_edge, True), edge, [in_vmem] * 2)(part, got_far)
    got_far = lax.ppermute(far, "dom", far_pairs)
    part = call(
        second_kernel,
        block,
        [in_vmem] * 10,
        scratch + [pltpu.VMEM(orbitals.shape, f32)],
        flops=3_000_000_000,
    )(*fields, strength, rowhot, zhot, near, far, part)

    def halves(count):
        return jax.ShapeDtypeStruct((orbs, 2 * count, wide // 2, deep), f32)

    def swap(chunks):
        return {
            k: lax.ppermute(chunks[k], "orb", [(i, i ^ k) for i in range(orb_devices)])
            for k in (2, 3, 1)
        }

    def rows_of(chunk):
        return [pltpu.VMEM((chunk.shape[1], orbs * orb_devices) + chunk.shape[2:], f32)]

    def chunk(count):
        return jax.ShapeDtypeStruct((orbs, 2 * count // orb_devices, wide // 2, deep), f32)

    row = jax.ShapeDtypeStruct((1, 128), f32)
    inner = layers - RADIUS
    near, *sends = call(second_near, (halves(inner),) + (chunk(inner),) * 4, [in_vmem] * 2)(
        part, got_near
    )
    own_near, got_early = sends[0], swap(sends)
    far, *sends = call(second_far, (halves(RADIUS),) + (chunk(RADIUS),) * 4, [in_vmem] * 2)(
        part, got_far
    )
    own_far, got_late = sends[0], swap(sends)
    early = call(near_gram, row, [in_vmem] * 4, rows_of(own_near), flops=1_000_000_000)(
        got_early[2], got_early[3], got_early[1], own_near
    )
    filtered, others = call(own_gram, (block, row), [in_vmem] * 3, flops=1_500_000_000)(
        early, near, far
    )
    terms = call(
        far_gram,
        jax.ShapeDtypeStruct((doms * orb_devices, 1, 128), f32),
        [in_vmem] * 5,
        rows_of(own_far),
    )(others, got_late[2], got_late[3], got_late[1], own_far)
    terms = lax.all_to_all(terms, ("dom", "orb"), 0, 0)
    gram = call(
        functools.partial(final_kernel, float(layers * wide * deep * doms)),
        jax.ShapeDtypeStruct((16, 16), f32),
        [in_vmem],
    )(terms)
    return filtered, gram


def solution(mesh):
    placed = (
        P("orb", "dom", None, None),
        P("dom", None, None),
        P("dom", None),
        P("dom", None, None),
        P("dom"),
        P("dom"),
        P(),
    )
    return jax.shard_map(
        on_device,
        mesh=mesh,
        in_specs=placed,
        out_specs=(P("orb", "dom", None, None), P()),
        check_vma=False,
    )
```

```python
import functools

import jax
import jax.numpy as jnp
from jax import lax
from jax.experimental import pallas as pl
from jax.experimental.pallas import tpu as pltpu
from jax.sharding import PartitionSpec as P

RADIUS = 6
STENCIL = (
    -5369.0 / 1800.0,
    12.0 / 7.0,
    -15.0 / 56.0,
    10.0 / 189.0,
    -1.0 / 112.0,
    2.0 / 1925.0,
    -1.0 / 16632.0,
)
LOWER_EDGE = 2.0
UPPER_EDGE = 17.0
MID_POINT = 0.5 * (UPPER_EDGE + LOWER_EDGE)
HALF_WIDTH = 0.5 * (UPPER_EDGE - LOWER_EDGE)
VMEM = pltpu.VMEM
NT = (((1,), (1,)), ((), ()))


def split(values):
    high = values.astype(jnp.bfloat16)
    return high, (values - high.astype(jnp.float32)).astype(jnp.bfloat16)


def place(condition):
    return jnp.where(condition, 1.0, 0.0).astype(jnp.bfloat16)


def mark_cells(index, rowhot, zhot):
    cells = index[...]
    row_of = cells >> 7
    lane_of = cells & 127
    row_iota = lax.broadcasted_iota(jnp.int32, (256, 128), 0)
    for a in range(cells.shape[0]):
        at = slice(a * 128, (a + 1) * 128)
        rowhot[:, at] = place(row_iota == row_of[a : a + 1])
        zhot[:, at] = place(row_iota[:128] == lane_of[a : a + 1])


def nonlocal_rows(load_rows, orbs, index, projector, strength, parts, rowhot, zhot, picked, spread):
    lanes = 128
    atoms, channels = projector.shape[0], projector.shape[1]
    for o in range(orbs):
        high, low = split(load_rows(o).T)
        parts[0, o * lanes : (o + 1) * lanes, :] = high
        parts[1, o * lanes : (o + 1) * lanes, :] = low
    cells = index[...]
    lane_of = cells & 127
    lane_iota = lax.broadcasted_iota(jnp.int32, (lanes, lanes), 0)
    for a in range(0, atoms, 2):
        at = slice(a * lanes, (a + 2) * lanes)
        found = jnp.dot(parts[0], rowhot[:, at], preferred_element_type=jnp.float32)
        found = found + jnp.dot(parts[1], rowhot[:, at], preferred_element_type=jnp.float32)
        for b in range(2):
            hot = lane_iota == lane_of[a + b : a + b + 1]
            for o in range(orbs):
                block = found[o * lanes : (o + 1) * lanes, b * lanes : (b + 1) * lanes]
                picked[o, a + b : a + b + 1, :] = jnp.sum(
                    jnp.where(hot, block, 0.0), axis=0, keepdims=True
                )
    inside = cells >= 0
    total = [jnp.zeros((atoms, lanes), jnp.float32) for _ in range(orbs)]
    for p in range(channels):
        shape = projector[:, p, :]
        for o in range(orbs):
            coefficient = jnp.sum(shape * picked[o], axis=1, keepdims=True)
            total[o] = total[o] + shape * (coefficient * strength[p])
    for o in range(orbs):
        high, low = split(jnp.where(inside, total[o], 0.0))
        for a in range(atoms):
            at = slice(a * lanes, (a + 1) * lanes)
            hot = zhot[:, at]
            spread[0, o * lanes : (o + 1) * lanes, at] = hot * high[a : a + 1]
            spread[1, o * lanes : (o + 1) * lanes, at] = hot * low[a : a + 1]
    out = lax.dot_general(rowhot[...], spread[0], NT, preferred_element_type=jnp.float32)
    return out + lax.dot_general(rowhot[...], spread[1], NT, preferred_element_type=jnp.float32)


def local_layer(load, potential, i, layers):
    centre = load(i)
    total = (potential - (1.5 * STENCIL[0] + MID_POINT)) * centre
    for k in range(1, RADIUS + 1):
        near = pltpu.roll(centre, k, 0) + pltpu.roll(centre, centre.shape[0] - k, 0)
        near = near + pltpu.roll(centre, k, 1) + pltpu.roll(centre, centre.shape[1] - k, 1)
        if i - k >= 0:
            near = near + load(i - k)
        if i + k < layers:
            near = near + load(i + k)
        total = total - (0.5 * STENCIL[k]) * near
    return total


def first_kernel(
    species,
    count,
    energy,
    v,
    potential,
    index,
    projector,
    far,
    near,
    out,
    rowhot,
    zhot,
    strength,
    parts,
    picked,
    spread,
):
    orbs, layers = v.shape[0], v.shape[1]
    slot_strengths(species, count, energy, strength)
    mark_cells(index, rowhot, zhot)
    hat = nonlocal_rows(
        lambda o: v[o].reshape(256, 128),
        orbs,
        index,
        projector,
        strength,
        parts,
        rowhot,
        zhot,
        picked,
        spread,
    )
    for o in range(orbs):
        for i in range(layers):
            total = local_layer(lambda j: v[o, j], potential[i], i, layers)
            total = total + hat[i * 16 : (i + 1) * 16, o * 128 : (o + 1) * 128]
            out[o, i] = total * (1.0 / HALF_WIDTH)
    cut_edges(out, far, near)


def second_kernel(
    v,
    potential,
    index,
    projector,
    strength,
    rowhot,
    zhot,
    near,
    far,
    part,
    out,
    parts,
    picked,
    spread,
    held,
):
    orbs, layers = v.shape[0], v.shape[1]
    held[:, RADIUS : layers - RADIUS] = part[:, RADIUS : layers - RADIUS]

    def edges(below, above):
        low, high = held.at[:, :RADIUS], held.at[:, layers - RADIUS :]
        add_below(part.at[:, :RADIUS], below, low, -0.5 / HALF_WIDTH)
        add_above(part.at[:, layers - RADIUS :], above, high, -0.5 / HALF_WIDTH)

    by_parity(edges, far, near)
    hat = nonlocal_rows(
        lambda o: held[o].reshape(256, 128),
        orbs,
        index,
        projector,
        strength,
        parts,
        rowhot,
        zhot,
        picked,
        spread,
    )
    for o in range(orbs):
        for i in range(layers):
            total = local_layer(lambda j: held[o, j], potential[i], i, layers)
            total = total + hat[i * 16 : (i + 1) * 16, o * 128 : (o + 1) * 128]
            out[o, i] = total * (2.0 / HALF_WIDTH) - v[o, i]


def from_below(below, o, i):
    total = STENCIL[i + 1] * below[o, RADIUS - 1]
    for k in range(i + 2, RADIUS + 1):
        total = total + STENCIL[k] * below[o, RADIUS + i - k]
    return total


def from_above(above, o, j):
    total = STENCIL[j + 1] * above[o, 0]
    for k in range(j + 2, RADIUS + 1):
        total = total + STENCIL[k] * above[o, k - j - 1]
    return total


def far_near_starts(layers):
    odd = lax.axis_index("dom") & 1
    first = odd * (layers - RADIUS)
    return first, layers - RADIUS - first


def by_parity(body, far, near):
    odd = lax.axis_index("dom") & 1

    @pl.when(odd == 0)
    def _():
        body(far, near)

    @pl.when(odd == 1)
    def _():
        body(near, far)


def order_edges(low, high, far, near):
    def body(far_edge, near_edge):
        far[...] = far_edge[...]
        near[...] = near_edge[...]

    by_parity(body, low, high)


def cut_edges(block, far, near):
    first, last = far_near_starts(block.shape[1])
    for o in range(block.shape[0]):
        far[o] = block[o, pl.ds(first, RADIUS)]
        near[o] = block[o, pl.ds(last, RADIUS)]


def add_below(low, below, out, scale):
    for o in range(low.shape[0]):
        for i in range(RADIUS):
            out[o, i] = low[o, i] + scale * from_below(below, o, i)


def add_above(high, above, out, scale):
    for o in range(high.shape[0]):
        for i in range(RADIUS):
            at = RADIUS - 1 - i
            out[o, at] = high[o, at] + scale * from_above(above, o, i)


def slot_strengths(species, count, energy, strength):
    channels, atoms = strength.shape[0], strength.shape[1]
    slot = lax.broadcasted_iota(jnp.int32, (atoms, 128), 0)
    live = slot < count[0]
    for p in range(channels):
        total = jnp.zeros((atoms, 128), jnp.float32)
        for a in range(atoms):
            total = jnp.where(slot == a, energy[species[a], p], total)
        strength[p] = jnp.where(live, total, 0.0)


def deal(block, chunks):
    me = lax.axis_index("orb")
    depth = chunks[0].shape[1]
    for k, chunk in enumerate(chunks):
        first = (me ^ k) * depth
        for o in range(block.shape[0]):
            chunk[o] = block[o, pl.ds(first, depth)]


def as_halves(rows):
    return rows.reshape(rows.shape[0], 2 * rows.shape[1], 8, 128)


def second_near(part, v, got, block, *scratch):
    (*chunks, halo, edge) = scratch
    layers = part.shape[1]
    inner = layers - RADIUS
    odd = lax.axis_index("dom") & 1
    one, two = -0.5 / HALF_WIDTH, -1.0 / HALF_WIDTH

    @pl.when(odd == 0)
    def _():
        add_below(got, v.at[:, inner:], halo, one)
        add_above(part.at[:, inner:], halo, edge, two)
        block[:, : 2 * (inner - RADIUS)] = as_halves(part[:, RADIUS:inner])
        block[:, 2 * (inner - RADIUS) :] = as_halves(edge[...])

    @pl.when(odd == 1)
    def _():
        add_above(got, v.at[:, :RADIUS], halo, one)
        add_below(part.at[:, :RADIUS], halo, edge, two)
        block[:, : 2 * RADIUS] = as_halves(edge[...])
        block[:, 2 * RADIUS :] = as_halves(part[:, RADIUS:inner])

    deal(block, chunks)


def second_far(part, v, got, block, *scratch):
    (*chunks, halo, edge) = scratch
    layers = part.shape[1]
    inner = layers - RADIUS
    odd = lax.axis_index("dom") & 1
    one, two = -0.5 / HALF_WIDTH, -1.0 / HALF_WIDTH

    @pl.when(odd == 0)
    def _():
        add_above(got, v.at[:, :RADIUS], halo, one)
        add_below(part.at[:, :RADIUS], halo, edge, two)

    @pl.when(odd == 1)
    def _():
        add_below(got, v.at[:, inner:], halo, one)
        add_above(part.at[:, inner:], halo, edge, two)

    block[...] = as_halves(edge[...])
    deal(block, chunks)


def split_3(values):
    high = values.astype(jnp.bfloat16)
    rest = values - high.astype(jnp.float32)
    middle = rest.astype(jnp.bfloat16)
    low = (rest - middle.astype(jnp.float32)).astype(jnp.bfloat16)
    return jnp.concatenate([high, middle, low], axis=0)


def lane_block(lane):
    block = lane >> 4
    first = jnp.where(block < 3, 0, jnp.where(block < 5, 1, 2))
    second = jnp.where(block < 3, block + 1, jnp.where(block < 5, block - 1, 3))
    return block, 4 * first + ((lane >> 2) & 3), 4 * second + (lane & 3)


def row_products(loads, rows, left_rows, right_rows):
    total = None
    for load in loads:
        high, low = split(load().reshape(rows, 128))
        left = jnp.concatenate([high, high, low], axis=1)[left_rows]
        right = jnp.concatenate([high, low, high], axis=1)[right_rows]
        term = lax.dot_general(left, right, NT, preferred_element_type=jnp.float32)
        total = term if total is None else total + term
    row = lax.broadcasted_iota(jnp.int32, total.shape, 0)
    column = lax.broadcasted_iota(jnp.int32, total.shape, 1)
    total = jnp.where((row & 7) == (column & 7), total, 0.0)
    return jnp.sum(total.reshape(total.shape[0] // 8, 8, total.shape[1]), axis=1)


def pack(sums, column_orbital, row_orbital):
    count, columns = sums.shape
    lane = lax.broadcasted_iota(jnp.int32, (columns, 128), 1)
    orbital = lax.broadcasted_iota(jnp.int32, (columns, 128), 0) >> 3
    wide = jnp.dot(
        split_3(sums),
        place(orbital == column_orbital(lane)),
        preferred_element_type=jnp.float32,
    )
    wide = wide[:count] + wide[count : 2 * count] + wide[2 * count :]
    lane = lax.broadcasted_iota(jnp.int32, (count, 128), 1)
    orbital = lax.broadcasted_iota(jnp.int32, (count, 128), 0)
    return jnp.sum(jnp.where(orbital == row_orbital(lane), wide, 0.0), axis=0, keepdims=True)


def own_gram(early, near, far, out, own):
    orbs, layers = out.shape[0], out.shape[1]
    first, _ = far_near_starts(layers)
    rest = RADIUS - (first * RADIUS) // (layers - RADIUS)
    out[:, pl.ds(first, RADIUS)] = far[...].reshape(orbs, RADIUS, 16, 128)
    out[:, pl.ds(rest, layers - RADIUS)] = near[...].reshape(orbs, layers - RADIUS, 16, 128)
    everything = slice(None)
    loads = [lambda h=h: near[:, h] for h in range(near.shape[1])]
    loads += [lambda h=h: far[:, h] for h in range(far.shape[1])]
    sums = row_products(loads, 8 * orbs, everything, everything)
    sums = jnp.concatenate([sums, jnp.zeros_like(sums)], axis=0)
    lanes = pack(sums, lambda lane: lane & 3, lambda lane: (lane >> 2) & 3)
    lane = lax.broadcasted_iota(jnp.int32, (1, 128), 1)
    own[...] = early[...] + jnp.where((lane >= 96) & (lane < 112), lanes, 0.0)


def gram_lanes(chunks, rows):
    orbs, depth = chunks[0].shape[0], chunks[0].shape[1]
    me = lax.axis_index("orb")
    for k, chunk in enumerate(chunks):
        first = (me ^ k) * orbs
        for o in range(orbs):
            for h in range(depth):
                rows[h, first + o] = chunk[o, h]
    loads = [lambda h=h: rows[h] for h in range(depth)]
    sums = row_products(loads, 128, slice(0, 96), slice(32, 128))
    sums = jnp.concatenate([sums, jnp.zeros((4, 96), jnp.float32)], axis=0)
    lanes = pack(sums, lambda lane: lane_block(lane)[2] - 4, lambda lane: lane_block(lane)[1])
    lane = lax.broadcasted_iota(jnp.int32, (1, 128), 1)
    return jnp.where(lane < 96, lanes, 0.0)


def near_gram(got_2, got_3, got_1, own, out, rows):
    out[...] = gram_lanes((own, got_1, got_2, got_3), rows)


def far_gram(others, got_2, got_3, got_1, own, out, rows):
    lanes = gram_lanes((own, got_1, got_2, got_3), rows) + others[...]
    out[...] = jnp.broadcast_to(lanes[None], out.shape)


def final_kernel(cells, terms, out):
    orbs = 4
    sums = [terms[q] for q in range(orbs)]
    for d in range(1, terms.shape[0] // orbs):
        for q in range(orbs):
            sums[q] = sums[q] + terms[d * orbs + q]
    across = sums[0] + sums[1] + sums[2] + sums[3]
    row = lax.broadcasted_iota(jnp.int32, (16, 128), 0)
    lane = lax.broadcasted_iota(jnp.int32, (16, 128), 1)
    block, first, second = lane_block(lane)
    own = jnp.where(
        row < 8,
        jnp.where(row < 4, sums[0], sums[1]),
        jnp.where(row < 12, sums[2], sums[3]),
    )
    upper = jnp.where((block < 6) & (first == row), across, 0.0)
    lower = jnp.where((block < 6) & (second == row), across, 0.0)
    own = jnp.where((block == 6) & (((lane >> 2) & 3) == (row & 3)), own, 0.0)
    column = lax.broadcasted_iota(jnp.int32, (128, 16), 1)
    lane = lax.broadcasted_iota(jnp.int32, (128, 16), 0)
    block, first, second = lane_block(lane)

    def unpack(values, condition):
        parts = jnp.dot(split_3(values), place(condition), preferred_element_type=jnp.float32)
        return parts[:16] + parts[16:32] + parts[32:]

    total = unpack(upper, second == column) + unpack(lower, first == column)
    same = (lax.broadcasted_iota(jnp.int32, (16, 16), 0) >> 2) == (
        lax.broadcasted_iota(jnp.int32, (16, 16), 1) >> 2
    )
    total = total + jnp.where(same, unpack(own, (lane & 3) == (column & 3)), 0.0)
    out[...] = total * (1.0 / cells)


def call(kernel, outs, in_specs, scratch=(), flops=10_000_000, limit=48 * 2**20):
    return pl.pallas_call(
        kernel,
        out_shape=outs,
        in_specs=in_specs,
        out_specs=jax.tree.map(lambda _: pl.BlockSpec(memory_space=VMEM), outs),
        scratch_shapes=list(scratch),
        compiler_params=pltpu.CompilerParams(vmem_limit_bytes=limit),
        cost_estimate=pl.CostEstimate(flops=flops, bytes_accessed=2**21, transcendentals=0),
    )


def on_device(
    orbitals, local_potential, sphere_index, projector, species, atom_count, channel_energy
):
    f32 = jnp.float32
    in_vmem = pl.BlockSpec(memory_space=VMEM)
    orbs, layers, wide, deep = orbitals.shape
    doms, orb_devices = lax.axis_size("dom"), lax.axis_size("orb")
    far_pairs = [(i, (i - 1 if i % 2 == 0 else i + 1) % doms) for i in range(doms)]
    near_pairs = [(i, i ^ 1) for i in range(doms)]
    edge = jax.ShapeDtypeStruct((orbs, RADIUS, wide, deep), f32)
    block = jax.ShapeDtypeStruct(orbitals.shape, f32)
    atoms, points = sphere_index.shape
    in_smem = pl.BlockSpec(memory_space=pltpu.SMEM)
    scalars = (species, atom_count, channel_energy)
    fields = (orbitals, local_potential, sphere_index, projector)
    far, near = call(order_edges, (edge, edge), [in_vmem] * 2)(
        orbitals[:, :RADIUS], orbitals[:, layers - RADIUS :]
    )
    got_far = lax.ppermute(far, "dom", far_pairs)
    got_near = lax.ppermute(near, "dom", near_pairs)
    scratch = [
        pltpu.VMEM((2, orbs * deep, layers * wide), jnp.bfloat16),
        pltpu.VMEM((orbs,) + sphere_index.shape, f32),
        pltpu.VMEM((2, orbs * deep, atoms * points), jnp.bfloat16),
    ]
    far, near, part, rowhot, zhot, strength = call(
        first_kernel,
        (
            edge,
            edge,
            block,
            jax.ShapeDtypeStruct((layers * wide, atoms * points), jnp.bfloat16),
            jax.ShapeDtypeStruct((deep, atoms * points), jnp.bfloat16),
            jax.ShapeDtypeStruct((projector.shape[1], atoms, deep), f32),
        ),
        [in_smem] * 3 + [in_vmem] * 4,
        scratch,
        flops=3_000_000_000,
    )(*scalars, *fields)
    next_far = lax.ppermute(far, "dom", far_pairs)
    next_near = lax.ppermute(near, "dom", near_pairs)
    part = call(
        second_kernel,
        block,
        [in_vmem] * 10,
        scratch + [pltpu.VMEM(orbitals.shape, f32)],
        flops=3_000_000_000,
    )(*fields, strength, rowhot, zhot, got_near, got_far, part)

    def halves(count):
        return jax.ShapeDtypeStruct((orbs, 2 * count, wide // 2, deep), f32)

    def swap(chunks):
        return {
            k: lax.ppermute(chunks[k], "orb", [(i, i ^ k) for i in range(orb_devices)])
            for k in (2, 3, 1)
        }

    def rows_of(chunk):
        return [pltpu.VMEM((chunk.shape[1], orbs * orb_devices) + chunk.shape[2:], f32)]

    def chunk(count):
        return jax.ShapeDtypeStruct((orbs, 2 * count // orb_devices, wide // 2, deep), f32)

    row = jax.ShapeDtypeStruct((1, 128), f32)
    inner = layers - RADIUS
    edges = [pltpu.VMEM(edge.shape, f32)] * 2
    near, *sends = call(
        second_near, (halves(inner),) + (chunk(inner),) * 4, [in_vmem] * 3, edges
    )(part, orbitals, next_near)
    own_near, got_early = sends[0], swap(sends)
    far, *sends = call(
        second_far, (halves(RADIUS),) + (chunk(RADIUS),) * 4, [in_vmem] * 3, edges
    )(part, orbitals, next_far)
    own_far, got_late = sends[0], swap(sends)
    early = call(near_gram, row, [in_vmem] * 4, rows_of(own_near), flops=1_000_000_000)(
        got_early[2], got_early[3], got_early[1], own_near
    )
    filtered, others = call(own_gram, (block, row), [in_vmem] * 3, flops=1_500_000_000)(
        early, near, far
    )
    terms = call(
        far_gram,
        jax.ShapeDtypeStruct((doms * orb_devices, 1, 128), f32),
        [in_vmem] * 5,
        rows_of(own_far),
    )(others, got_late[2], got_late[3], got_late[1], own_far)
    terms = lax.all_to_all(terms, ("dom", "orb"), 0, 0)
    gram = call(
        functools.partial(final_kernel, float(layers * wide * deep * doms)),
        jax.ShapeDtypeStruct((16, 16), f32),
        [in_vmem],
    )(terms)
    return filtered, gram


def solution(mesh):
    placed = (
        P("orb", "dom", None, None),
        P("dom", None, None),
        P("dom", None),
        P("dom", None, None),
        P("dom"),
        P("dom"),
        P(),
    )
    return jax.shard_map(
        on_device,
        mesh=mesh,
        in_specs=placed,
        out_specs=(P("orb", "dom", None, None), P()),
        check_vma=False,
    )
```

```python
import functools

import jax
import jax.numpy as jnp
from jax import lax
from jax.experimental import pallas as pl
from jax.experimental.pallas import tpu as pltpu
from jax.sharding import PartitionSpec as P

RADIUS = 6
STENCIL = (
    -5369.0 / 1800.0,
    12.0 / 7.0,
    -15.0 / 56.0,
    10.0 / 189.0,
    -1.0 / 112.0,
    2.0 / 1925.0,
    -1.0 / 16632.0,
)
LOWER_EDGE = 2.0
UPPER_EDGE = 17.0
MID_POINT = 0.5 * (UPPER_EDGE + LOWER_EDGE)
HALF_WIDTH = 0.5 * (UPPER_EDGE - LOWER_EDGE)
VMEM = pltpu.VMEM
NT = (((1,), (1,)), ((), ()))


def split(values):
    high = values.astype(jnp.bfloat16)
    return high, (values - high.astype(jnp.float32)).astype(jnp.bfloat16)


def place(condition):
    return jnp.where(condition, 1.0, 0.0).astype(jnp.bfloat16)


def mark_cells(index, rowhot, zhot):
    cells = index[...]
    row_of = cells >> 7
    lane_of = cells & 127
    row_iota = lax.broadcasted_iota(jnp.int32, (256, 128), 0)
    for a in range(cells.shape[0]):
        at = slice(a * 128, (a + 1) * 128)
        rowhot[:, at] = place(row_iota == row_of[a : a + 1])
        zhot[:, at] = place(row_iota[:128] == lane_of[a : a + 1])


def nonlocal_rows(load_rows, orbs, index, projector, strength, parts, rowhot, zhot, picked, spread):
    lanes = 128
    atoms, channels = projector.shape[0], projector.shape[1]
    for o in range(orbs):
        high, low = split(load_rows(o).T)
        parts[0, o * lanes : (o + 1) * lanes, :] = high
        parts[1, o * lanes : (o + 1) * lanes, :] = low
    cells = index[...]
    lane_of = cells & 127
    lane_iota = lax.broadcasted_iota(jnp.int32, (lanes, lanes), 0)
    for a in range(0, atoms, 2):
        at = slice(a * lanes, (a + 2) * lanes)
        found = jnp.dot(parts[0], rowhot[:, at], preferred_element_type=jnp.float32)
        found = found + jnp.dot(parts[1], rowhot[:, at], preferred_element_type=jnp.float32)
        for b in range(2):
            hot = lane_iota == lane_of[a + b : a + b + 1]
            for o in range(orbs):
                block = found[o * lanes : (o + 1) * lanes, b * lanes : (b + 1) * lanes]
                picked[o, a + b : a + b + 1, :] = jnp.sum(
                    jnp.where(hot, block, 0.0), axis=0, keepdims=True
                )
    inside = cells >= 0
    total = [jnp.zeros((atoms, lanes), jnp.float32) for _ in range(orbs)]
    for p in range(channels):
        shape = projector[:, p, :]
        for o in range(orbs):
            coefficient = jnp.sum(shape * picked[o], axis=1, keepdims=True)
            total[o] = total[o] + shape * (coefficient * strength[p])
    for o in range(orbs):
        high, low = split(jnp.where(inside, total[o], 0.0))
        for a in range(atoms):
            at = slice(a * lanes, (a + 1) * lanes)
            hot = zhot[:, at]
            spread[0, o * lanes : (o + 1) * lanes, at] = hot * high[a : a + 1]
            spread[1, o * lanes : (o + 1) * lanes, at] = hot * low[a : a + 1]
    out = lax.dot_general(rowhot[...], spread[0], NT, preferred_element_type=jnp.float32)
    return out + lax.dot_general(rowhot[...], spread[1], NT, preferred_element_type=jnp.float32)


def local_layer(load, potential, i, layers):
    centre = load(i)
    total = (potential - (1.5 * STENCIL[0] + MID_POINT)) * centre
    for k in range(1, RADIUS + 1):
        near = pltpu.roll(centre, k, 0) + pltpu.roll(centre, centre.shape[0] - k, 0)
        near = near + pltpu.roll(centre, k, 1) + pltpu.roll(centre, centre.shape[1] - k, 1)
        if i - k >= 0:
            near = near + load(i - k)
        if i + k < layers:
            near = near + load(i + k)
        total = total - (0.5 * STENCIL[k]) * near
    return total


def first_kernel(
    species,
    count,
    energy,
    v,
    potential,
    index,
    projector,
    far,
    near,
    out,
    rowhot,
    zhot,
    strength,
    parts,
    picked,
    spread,
):
    orbs, layers = v.shape[0], v.shape[1]
    slot_strengths(species, count, energy, strength)
    mark_cells(index, rowhot, zhot)
    hat = nonlocal_rows(
        lambda o: v[o].reshape(256, 128),
        orbs,
        index,
        projector,
        strength,
        parts,
        rowhot,
        zhot,
        picked,
        spread,
    )
    for o in range(orbs):
        for i in range(layers):
            total = local_layer(lambda j: v[o, j], potential[i], i, layers)
            total = total + hat[i * 16 : (i + 1) * 16, o * 128 : (o + 1) * 128]
            out[o, i] = total * (1.0 / HALF_WIDTH)
    cut_edges(out, far, near)


def second_kernel(
    v,
    potential,
    index,
    projector,
    strength,
    rowhot,
    zhot,
    near,
    far,
    part,
    out,
    parts,
    picked,
    spread,
    held,
):
    orbs, layers = v.shape[0], v.shape[1]
    held[:, RADIUS : layers - RADIUS] = part[:, RADIUS : layers - RADIUS]

    def edges(below, above):
        low, high = held.at[:, :RADIUS], held.at[:, layers - RADIUS :]
        add_below(part.at[:, :RADIUS], below, low, -0.5 / HALF_WIDTH)
        add_above(part.at[:, layers - RADIUS :], above, high, -0.5 / HALF_WIDTH)

    by_parity(edges, far, near)
    hat = nonlocal_rows(
        lambda o: held[o].reshape(256, 128),
        orbs,
        index,
        projector,
        strength,
        parts,
        rowhot,
        zhot,
        picked,
        spread,
    )
    for o in range(orbs):
        for i in range(layers):
            total = local_layer(lambda j: held[o, j], potential[i], i, layers)
            total = total + hat[i * 16 : (i + 1) * 16, o * 128 : (o + 1) * 128]
            out[o, i] = total * (2.0 / HALF_WIDTH) - v[o, i]


def from_below(below, o, i):
    total = STENCIL[i + 1] * below[o, RADIUS - 1]
    for k in range(i + 2, RADIUS + 1):
        total = total + STENCIL[k] * below[o, RADIUS + i - k]
    return total


def from_above(above, o, j):
    total = STENCIL[j + 1] * above[o, 0]
    for k in range(j + 2, RADIUS + 1):
        total = total + STENCIL[k] * above[o, k - j - 1]
    return total


def far_near_starts(layers):
    odd = lax.axis_index("dom") & 1
    first = odd * (layers - RADIUS)
    return first, layers - RADIUS - first


def by_parity(body, far, near):
    odd = lax.axis_index("dom") & 1

    @pl.when(odd == 0)
    def _():
        body(far, near)

    @pl.when(odd == 1)
    def _():
        body(near, far)


def order_edges(low, high, far, near):
    def body(far_edge, near_edge):
        far[...] = far_edge[...]
        near[...] = near_edge[...]

    by_parity(body, low, high)


def cut_edges(block, far, near):
    first, last = far_near_starts(block.shape[1])
    for o in range(block.shape[0]):
        far[o] = block[o, pl.ds(first, RADIUS)]
        near[o] = block[o, pl.ds(last, RADIUS)]


def add_below(low, below, out, scale):
    for o in range(low.shape[0]):
        for i in range(RADIUS):
            out[o, i] = low[o, i] + scale * from_below(below, o, i)


def add_above(high, above, out, scale):
    for o in range(high.shape[0]):
        for i in range(RADIUS):
            at = RADIUS - 1 - i
            out[o, at] = high[o, at] + scale * from_above(above, o, i)


def slot_strengths(species, count, energy, strength):
    channels, atoms = strength.shape[0], strength.shape[1]
    slot = lax.broadcasted_iota(jnp.int32, (atoms, atoms), 0)
    lane = lax.broadcasted_iota(jnp.int32, (atoms, atoms), 1)
    kinds = species[...].astype(jnp.float32).reshape(1, atoms)
    kinds = jnp.sum(jnp.where(slot == lane, kinds, 0.0), axis=1, keepdims=True)
    kinds = jnp.broadcast_to(kinds, (atoms, 128))
    slot = lax.broadcasted_iota(jnp.int32, (atoms, 128), 0)
    live = slot < count[...].reshape(1, 1)
    for p in range(channels):
        total = jnp.zeros((atoms, 128), jnp.float32)
        for kind in range(energy.shape[0]):
            total = jnp.where(kinds == float(kind), energy[kind : kind + 1, p : p + 1], total)
        strength[p] = jnp.where(live, total, 0.0)


def deal(block, chunks):
    me = lax.axis_index("orb")
    depth = chunks[0].shape[1]
    for k, chunk in enumerate(chunks):
        first = (me ^ k) * depth
        for o in range(block.shape[0]):
            chunk[o] = block[o, pl.ds(first, depth)]


def as_halves(rows):
    return rows.reshape(rows.shape[0], 2 * rows.shape[1], 8, 128)


def second_near(part, v, got, block, *scratch):
    (*chunks, halo, edge) = scratch
    layers = part.shape[1]
    inner = layers - RADIUS
    odd = lax.axis_index("dom") & 1
    one, two = -0.5 / HALF_WIDTH, -1.0 / HALF_WIDTH

    @pl.when(odd == 0)
    def _():
        add_below(got, v.at[:, inner:], halo, one)
        add_above(part.at[:, inner:], halo, edge, two)
        block[:, : 2 * (inner - RADIUS)] = as_halves(part[:, RADIUS:inner])
        block[:, 2 * (inner - RADIUS) :] = as_halves(edge[...])

    @pl.when(odd == 1)
    def _():
        add_above(got, v.at[:, :RADIUS], halo, one)
        add_below(part.at[:, :RADIUS], halo, edge, two)
        block[:, : 2 * RADIUS] = as_halves(edge[...])
        block[:, 2 * RADIUS :] = as_halves(part[:, RADIUS:inner])

    deal(block, chunks)


def second_far(part, v, got, block, *scratch):
    (*chunks, halo, edge) = scratch
    layers = part.shape[1]
    inner = layers - RADIUS
    odd = lax.axis_index("dom") & 1
    one, two = -0.5 / HALF_WIDTH, -1.0 / HALF_WIDTH

    @pl.when(odd == 0)
    def _():
        add_above(got, v.at[:, :RADIUS], halo, one)
        add_below(part.at[:, :RADIUS], halo, edge, two)

    @pl.when(odd == 1)
    def _():
        add_below(got, v.at[:, inner:], halo, one)
        add_above(part.at[:, inner:], halo, edge, two)

    block[...] = as_halves(edge[...])
    deal(block, chunks)


def split_3(values):
    high = values.astype(jnp.bfloat16)
    rest = values - high.astype(jnp.float32)
    middle = rest.astype(jnp.bfloat16)
    low = (rest - middle.astype(jnp.float32)).astype(jnp.bfloat16)
    return jnp.concatenate([high, middle, low], axis=0)


def lane_block(lane):
    block = lane >> 4
    first = jnp.where(block < 3, 0, jnp.where(block < 5, 1, 2))
    second = jnp.where(block < 3, block + 1, jnp.where(block < 5, block - 1, 3))
    return block, 4 * first + ((lane >> 2) & 3), 4 * second + (lane & 3)


def row_products(loads, rows, left_rows, right_rows):
    left, right = [], []
    for load in loads:
        high, low = split(load().reshape(rows, 128))
        left += [high, high, low]
        right += [high, low, high]
    total = lax.dot_general(
        jnp.concatenate(left, axis=1)[left_rows],
        jnp.concatenate(right, axis=1)[right_rows],
        NT,
        preferred_element_type=jnp.float32,
    )
    row = lax.broadcasted_iota(jnp.int32, total.shape, 0)
    column = lax.broadcasted_iota(jnp.int32, total.shape, 1)
    total = jnp.where((row & 7) == (column & 7), total, 0.0)
    return jnp.sum(total.reshape(total.shape[0] // 8, 8, total.shape[1]), axis=1)


def pack(sums, column_orbital, row_orbital):
    count, columns = sums.shape
    lane = lax.broadcasted_iota(jnp.int32, (columns, 128), 1)
    orbital = lax.broadcasted_iota(jnp.int32, (columns, 128), 0) >> 3
    wide = jnp.dot(
        split_3(sums),
        place(orbital == column_orbital(lane)),
        preferred_element_type=jnp.float32,
    )
    wide = wide[:count] + wide[count : 2 * count] + wide[2 * count :]
    lane = lax.broadcasted_iota(jnp.int32, (count, 128), 1)
    orbital = lax.broadcasted_iota(jnp.int32, (count, 128), 0)
    return jnp.sum(jnp.where(orbital == row_orbital(lane), wide, 0.0), axis=0, keepdims=True)


def own_gram(early, near, far, out, own):
    orbs, layers = out.shape[0], out.shape[1]
    first, _ = far_near_starts(layers)
    rest = RADIUS - (first * RADIUS) // (layers - RADIUS)
    out[:, pl.ds(first, RADIUS)] = far[...].reshape(orbs, RADIUS, 16, 128)
    out[:, pl.ds(rest, layers - RADIUS)] = near[...].reshape(orbs, layers - RADIUS, 16, 128)
    everything = slice(None)
    loads = [lambda h=h: near[:, h] for h in range(near.shape[1])]
    loads += [lambda h=h: far[:, h] for h in range(far.shape[1])]
    sums = row_products(loads, 8 * orbs, everything, everything)
    sums = jnp.concatenate([sums, jnp.zeros_like(sums)], axis=0)
    lanes = pack(sums, lambda lane: lane & 3, lambda lane: (lane >> 2) & 3)
    lane = lax.broadcasted_iota(jnp.int32, (1, 128), 1)
    own[...] = early[...] + jnp.where((lane >= 96) & (lane < 112), lanes, 0.0)


def gram_lanes(chunks, rows):
    orbs, depth = chunks[0].shape[0], chunks[0].shape[1]
    me = lax.axis_index("orb")
    for k, chunk in enumerate(chunks):
        first = (me ^ k) * orbs
        for o in range(orbs):
            for h in range(depth):
                rows[h, first + o] = chunk[o, h]
    loads = [lambda h=h: rows[h] for h in range(depth)]
    sums = row_products(loads, 128, slice(0, 96), slice(32, 128))
    sums = jnp.concatenate([sums, jnp.zeros((4, 96), jnp.float32)], axis=0)
    lanes = pack(sums, lambda lane: lane_block(lane)[2] - 4, lambda lane: lane_block(lane)[1])
    lane = lax.broadcasted_iota(jnp.int32, (1, 128), 1)
    return jnp.where(lane < 96, lanes, 0.0)


def near_gram(got_2, got_3, got_1, own, out, rows):
    out[...] = gram_lanes((own, got_1, got_2, got_3), rows)


def far_gram(others, got_2, got_3, got_1, own, out, rows):
    lanes = gram_lanes((own, got_1, got_2, got_3), rows) + others[...]
    out[...] = jnp.broadcast_to(lanes[None], out.shape)


def final_kernel(cells, terms, out):
    orbs = 4
    sums = [terms[q] for q in range(orbs)]
    for d in range(1, terms.shape[0] // orbs):
        for q in range(orbs):
            sums[q] = sums[q] + terms[d * orbs + q]
    across = sums[0] + sums[1] + sums[2] + sums[3]
    row = lax.broadcasted_iota(jnp.int32, (16, 128), 0)
    lane = lax.broadcasted_iota(jnp.int32, (16, 128), 1)
    block, first, second = lane_block(lane)
    own = jnp.where(
        row < 8,
        jnp.where(row < 4, sums[0], sums[1]),
        jnp.where(row < 12, sums[2], sums[3]),
    )
    upper = jnp.where((block < 6) & (first == row), across, 0.0)
    lower = jnp.where((block < 6) & (second == row), across, 0.0)
    own = jnp.where((block == 6) & (((lane >> 2) & 3) == (row & 3)), own, 0.0)
    column = lax.broadcasted_iota(jnp.int32, (128, 16), 1)
    lane = lax.broadcasted_iota(jnp.int32, (128, 16), 0)
    block, first, second = lane_block(lane)

    def unpack(values, condition):
        parts = jnp.dot(split_3(values), place(condition), preferred_element_type=jnp.float32)
        return parts[:16] + parts[16:32] + parts[32:]

    total = unpack(upper, second == column) + unpack(lower, first == column)
    same = (lax.broadcasted_iota(jnp.int32, (16, 16), 0) >> 2) == (
        lax.broadcasted_iota(jnp.int32, (16, 16), 1) >> 2
    )
    total = total + jnp.where(same, unpack(own, (lane & 3) == (column & 3)), 0.0)
    out[...] = total * (1.0 / cells)


def call(kernel, outs, in_specs, scratch=(), flops=10_000_000, limit=48 * 2**20):
    return pl.pallas_call(
        kernel,
        out_shape=outs,
        in_specs=in_specs,
        out_specs=jax.tree.map(lambda _: pl.BlockSpec(memory_space=VMEM), outs),
        scratch_shapes=list(scratch),
        compiler_params=pltpu.CompilerParams(vmem_limit_bytes=limit),
        cost_estimate=pl.CostEstimate(flops=flops, bytes_accessed=2**21, transcendentals=0),
    )


def on_device(
    orbitals, local_potential, sphere_index, projector, species, atom_count, channel_energy
):
    f32 = jnp.float32
    in_vmem = pl.BlockSpec(memory_space=VMEM)
    orbs, layers, wide, deep = orbitals.shape
    doms, orb_devices = lax.axis_size("dom"), lax.axis_size("orb")
    far_pairs = [(i, (i - 1 if i % 2 == 0 else i + 1) % doms) for i in range(doms)]
    near_pairs = [(i, i ^ 1) for i in range(doms)]
    edge = jax.ShapeDtypeStruct((orbs, RADIUS, wide, deep), f32)
    block = jax.ShapeDtypeStruct(orbitals.shape, f32)
    atoms, points = sphere_index.shape
    scalars = (species, atom_count, channel_energy)
    fields = (orbitals, local_potential, sphere_index, projector)
    far, near = call(order_edges, (edge, edge), [in_vmem] * 2)(
        orbitals[:, :RADIUS], orbitals[:, layers - RADIUS :]
    )
    got_far = lax.ppermute(far, "dom", far_pairs)
    got_near = lax.ppermute(near, "dom", near_pairs)
    scratch = [
        pltpu.VMEM((2, orbs * deep, layers * wide), jnp.bfloat16),
        pltpu.VMEM((orbs,) + sphere_index.shape, f32),
        pltpu.VMEM((2, orbs * deep, atoms * points), jnp.bfloat16),
    ]
    far, near, part, rowhot, zhot, strength = call(
        first_kernel,
        (
            edge,
            edge,
            block,
            jax.ShapeDtypeStruct((layers * wide, atoms * points), jnp.bfloat16),
            jax.ShapeDtypeStruct((deep, atoms * points), jnp.bfloat16),
            jax.ShapeDtypeStruct((projector.shape[1], atoms, deep), f32),
        ),
        [in_vmem] * 7,
        scratch,
        flops=3_000_000_000,
    )(*scalars, *fields)
    next_far = lax.ppermute(far, "dom", far_pairs)
    next_near = lax.ppermute(near, "dom", near_pairs)
    part = call(
        second_kernel,
        block,
        [in_vmem] * 10,
        scratch + [pltpu.VMEM(orbitals.shape, f32)],
        flops=3_000_000_000,
    )(*fields, strength, rowhot, zhot, got_near, got_far, part)

    def halves(count):
        return jax.ShapeDtypeStruct((orbs, 2 * count, wide // 2, deep), f32)

    def swap(chunks):
        return {
            k: lax.ppermute(chunks[k], "orb", [(i, i ^ k) for i in range(orb_devices)])
            for k in (2, 3, 1)
        }

    def rows_of(chunk):
        return [pltpu.VMEM((chunk.shape[1], orbs * orb_devices) + chunk.shape[2:], f32)]

    def chunk(count):
        return jax.ShapeDtypeStruct((orbs, 2 * count // orb_devices, wide // 2, deep), f32)

    row = jax.ShapeDtypeStruct((1, 128), f32)
    inner = layers - RADIUS
    edges = [pltpu.VMEM(edge.shape, f32)] * 2
    near, *sends = call(
        second_near, (halves(inner),) + (chunk(inner),) * 4, [in_vmem] * 3, edges
    )(part, orbitals, next_near)
    own_near, got_early = sends[0], swap(sends)
    far, *sends = call(
        second_far, (halves(RADIUS),) + (chunk(RADIUS),) * 4, [in_vmem] * 3, edges
    )(part, orbitals, next_far)
    own_far, got_late = sends[0], swap(sends)
    early = call(near_gram, row, [in_vmem] * 4, rows_of(own_near), flops=1_000_000_000)(
        got_early[2], got_early[3], got_early[1], own_near
    )
    filtered, others = call(own_gram, (block, row), [in_vmem] * 3, flops=1_500_000_000)(
        early, near, far
    )
    terms = call(
        far_gram,
        jax.ShapeDtypeStruct((doms * orb_devices, 1, 128), f32),
        [in_vmem] * 5,
        rows_of(own_far),
    )(others, got_late[2], got_late[3], got_late[1], own_far)
    terms = lax.all_to_all(terms, ("dom", "orb"), 0, 0)
    gram = call(
        functools.partial(final_kernel, float(layers * wide * deep * doms)),
        jax.ShapeDtypeStruct((16, 16), f32),
        [in_vmem],
    )(terms)
    return filtered, gram


def solution(mesh):
    placed = (
        P("orb", "dom", None, None),
        P("dom", None, None),
        P("dom", None),
        P("dom", None, None),
        P("dom"),
        P("dom"),
        P(),
    )
    return jax.shard_map(
        on_device,
        mesh=mesh,
        in_specs=placed,
        out_specs=(P("orb", "dom", None, None), P()),
        check_vma=False,
    )
```

```python
import functools

import jax
import jax.numpy as jnp
from jax import lax
from jax.experimental import pallas as pl
from jax.experimental.pallas import tpu as pltpu
from jax.sharding import PartitionSpec as P

RADIUS = 6
STENCIL = (
    -5369.0 / 1800.0,
    12.0 / 7.0,
    -15.0 / 56.0,
    10.0 / 189.0,
    -1.0 / 112.0,
    2.0 / 1925.0,
    -1.0 / 16632.0,
)
LOWER_EDGE = 2.0
UPPER_EDGE = 17.0
MID_POINT = 0.5 * (UPPER_EDGE + LOWER_EDGE)
HALF_WIDTH = 0.5 * (UPPER_EDGE - LOWER_EDGE)
VMEM = pltpu.VMEM
NT = (((1,), (1,)), ((), ()))


def split(values):
    high = values.astype(jnp.bfloat16)
    return high, (values - high.astype(jnp.float32)).astype(jnp.bfloat16)


def place(condition):
    return jnp.where(condition, 1.0, 0.0).astype(jnp.bfloat16)


def mark_cells(index, rowhot, zhot):
    cells = index[...]
    row_of = cells >> 7
    lane_of = cells & 127
    row_iota = lax.broadcasted_iota(jnp.int32, (256, 128), 0)
    for a in range(cells.shape[0]):
        at = slice(a * 128, (a + 1) * 128)
        rowhot[:, at] = place(row_iota == row_of[a : a + 1])
        zhot[:, at] = place(row_iota[:128] == lane_of[a : a + 1])


def nonlocal_rows(
    load_rows, beside, orbs, index, projector, strength, parts, rowhot, zhot, picked, spread
):
    lanes = 128
    atoms, channels = projector.shape[0], projector.shape[1]
    for o in range(orbs):
        high, low = split(load_rows(o).T)
        parts[0, o * lanes : (o + 1) * lanes, :] = high
        parts[1, o * lanes : (o + 1) * lanes, :] = low
    cells = index[...]
    lane_of = cells & 127
    lane_iota = lax.broadcasted_iota(jnp.int32, (lanes, lanes), 0)
    for a in range(0, atoms, 2):
        at = slice(a * lanes, (a + 2) * lanes)
        beside(a // 2, atoms // 2)
        found = jnp.dot(parts[0], rowhot[:, at], preferred_element_type=jnp.float32)
        found = found + jnp.dot(parts[1], rowhot[:, at], preferred_element_type=jnp.float32)
        for b in range(2):
            hot = lane_iota == lane_of[a + b : a + b + 1]
            for o in range(orbs):
                block = found[o * lanes : (o + 1) * lanes, b * lanes : (b + 1) * lanes]
                picked[o, a + b : a + b + 1, :] = jnp.sum(
                    jnp.where(hot, block, 0.0), axis=0, keepdims=True
                )
    inside = cells >= 0
    total = [jnp.zeros((atoms, lanes), jnp.float32) for _ in range(orbs)]
    for p in range(channels):
        shape = projector[:, p, :]
        for o in range(orbs):
            coefficient = jnp.sum(shape * picked[o], axis=1, keepdims=True)
            total[o] = total[o] + shape * (coefficient * strength[p])
    for o in range(orbs):
        high, low = split(jnp.where(inside, total[o], 0.0))
        for a in range(atoms):
            at = slice(a * lanes, (a + 1) * lanes)
            hot = zhot[:, at]
            spread[0, o * lanes : (o + 1) * lanes, at] = hot * high[a : a + 1]
            spread[1, o * lanes : (o + 1) * lanes, at] = hot * low[a : a + 1]
    out = lax.dot_general(rowhot[...], spread[0], NT, preferred_element_type=jnp.float32)
    return out + lax.dot_general(rowhot[...], spread[1], NT, preferred_element_type=jnp.float32)


def local_layer(load, potential, i, layers):
    centre = load(i)
    total = (potential - (1.5 * STENCIL[0] + MID_POINT)) * centre
    for k in range(1, RADIUS + 1):
        near = pltpu.roll(centre, k, 0) + pltpu.roll(centre, centre.shape[0] - k, 0)
        near = near + pltpu.roll(centre, k, 1) + pltpu.roll(centre, centre.shape[1] - k, 1)
        if i - k >= 0:
            near = near + load(i - k)
        if i + k < layers:
            near = near + load(i + k)
        total = total - (0.5 * STENCIL[k]) * near
    return total


def first_kernel(
    species,
    count,
    energy,
    v,
    potential,
    index,
    projector,
    far,
    near,
    out,
    rowhot,
    zhot,
    strength,
    parts,
    picked,
    spread,
):
    orbs, layers = v.shape[0], v.shape[1]
    slot_strengths(species, count, energy, strength)
    mark_cells(index, rowhot, zhot)

    def local_terms(step, steps):
        for n in range(step * orbs * layers // steps, (step + 1) * orbs * layers // steps):
            o, i = divmod(n, layers)
            out[o, i] = local_layer(lambda j: v[o, j], potential[i], i, layers)

    hat = nonlocal_rows(
        lambda o: v[o].reshape(256, 128),
        local_terms,
        orbs,
        index,
        projector,
        strength,
        parts,
        rowhot,
        zhot,
        picked,
        spread,
    )
    for o in range(orbs):
        for i in range(layers):
            total = out[o, i] + hat[i * 16 : (i + 1) * 16, o * 128 : (o + 1) * 128]
            out[o, i] = total * (1.0 / HALF_WIDTH)
    cut_edges(out, far, near)


def second_kernel(
    v,
    potential,
    index,
    projector,
    strength,
    rowhot,
    zhot,
    near,
    far,
    part,
    out,
    parts,
    picked,
    spread,
    held,
):
    orbs, layers = v.shape[0], v.shape[1]
    held[:, RADIUS : layers - RADIUS] = part[:, RADIUS : layers - RADIUS]

    def edges(below, above):
        low, high = held.at[:, :RADIUS], held.at[:, layers - RADIUS :]
        add_below(part.at[:, :RADIUS], below, low, -0.5 / HALF_WIDTH)
        add_above(part.at[:, layers - RADIUS :], above, high, -0.5 / HALF_WIDTH)

    by_parity(edges, far, near)

    def local_terms(step, steps):
        for n in range(step * orbs * layers // steps, (step + 1) * orbs * layers // steps):
            o, i = divmod(n, layers)
            out[o, i] = local_layer(lambda j: held[o, j], potential[i], i, layers)

    hat = nonlocal_rows(
        lambda o: held[o].reshape(256, 128),
        local_terms,
        orbs,
        index,
        projector,
        strength,
        parts,
        rowhot,
        zhot,
        picked,
        spread,
    )
    for o in range(orbs):
        for i in range(layers):
            total = out[o, i] + hat[i * 16 : (i + 1) * 16, o * 128 : (o + 1) * 128]
            out[o, i] = total * (2.0 / HALF_WIDTH) - v[o, i]


def from_below(below, o, i):
    total = STENCIL[i + 1] * below[o, RADIUS - 1]
    for k in range(i + 2, RADIUS + 1):
        total = total + STENCIL[k] * below[o, RADIUS + i - k]
    return total


def from_above(above, o, j):
    total = STENCIL[j + 1] * above[o, 0]
    for k in range(j + 2, RADIUS + 1):
        total = total + STENCIL[k] * above[o, k - j - 1]
    return total


def far_near_starts(layers):
    odd = lax.axis_index("dom") & 1
    first = odd * (layers - RADIUS)
    return first, layers - RADIUS - first


def by_parity(body, far, near):
    odd = lax.axis_index("dom") & 1

    @pl.when(odd == 0)
    def _():
        body(far, near)

    @pl.when(odd == 1)
    def _():
        body(near, far)


def order_edges(low, high, far, near):
    def body(far_edge, near_edge):
        far[...] = far_edge[...]
        near[...] = near_edge[...]

    by_parity(body, low, high)


def cut_edges(block, far, near):
    first, last = far_near_starts(block.shape[1])
    for o in range(block.shape[0]):
        far[o] = block[o, pl.ds(first, RADIUS)]
        near[o] = block[o, pl.ds(last, RADIUS)]


def add_below(low, below, out, scale):
    for o in range(low.shape[0]):
        for i in range(RADIUS):
            out[o, i] = low[o, i] + scale * from_below(below, o, i)


def add_above(high, above, out, scale):
    for o in range(high.shape[0]):
        for i in range(RADIUS):
            at = RADIUS - 1 - i
            out[o, at] = high[o, at] + scale * from_above(above, o, i)


def slot_strengths(species, count, energy, strength):
    channels, atoms = strength.shape[0], strength.shape[1]
    slot = lax.broadcasted_iota(jnp.int32, (atoms, atoms), 0)
    lane = lax.broadcasted_iota(jnp.int32, (atoms, atoms), 1)
    kinds = species[...].astype(jnp.float32).reshape(1, atoms)
    kinds = jnp.sum(jnp.where(slot == lane, kinds, 0.0), axis=1, keepdims=True)
    kinds = jnp.broadcast_to(kinds, (atoms, 128))
    slot = lax.broadcasted_iota(jnp.int32, (atoms, 128), 0)
    live = slot < count[...].reshape(1, 1)
    for p in range(channels):
        total = jnp.zeros((atoms, 128), jnp.float32)
        for kind in range(energy.shape[0]):
            total = jnp.where(kinds == float(kind), energy[kind : kind + 1, p : p + 1], total)
        strength[p] = jnp.where(live, total, 0.0)


def deal(block, chunks):
    me = lax.axis_index("orb")
    depth = chunks[0].shape[1]
    for k, chunk in enumerate(chunks):
        first = (me ^ k) * depth
        for o in range(block.shape[0]):
            chunk[o] = block[o, pl.ds(first, depth)]


def as_halves(rows):
    return rows.reshape(rows.shape[0], 2 * rows.shape[1], 8, 128)


def second_near(part, v, got, block, *scratch):
    (*chunks, halo, edge) = scratch
    layers = part.shape[1]
    inner = layers - RADIUS
    odd = lax.axis_index("dom") & 1
    one, two = -0.5 / HALF_WIDTH, -1.0 / HALF_WIDTH

    @pl.when(odd == 0)
    def _():
        add_below(got, v.at[:, inner:], halo, one)
        add_above(part.at[:, inner:], halo, edge, two)
        block[:, : 2 * (inner - RADIUS)] = as_halves(part[:, RADIUS:inner])
        block[:, 2 * (inner - RADIUS) :] = as_halves(edge[...])

    @pl.when(odd == 1)
    def _():
        add_above(got, v.at[:, :RADIUS], halo, one)
        add_below(part.at[:, :RADIUS], halo, edge, two)
        block[:, : 2 * RADIUS] = as_halves(edge[...])
        block[:, 2 * RADIUS :] = as_halves(part[:, RADIUS:inner])

    deal(block, chunks)


def second_far(part, v, got, block, *scratch):
    (*chunks, halo, edge) = scratch
    layers = part.shape[1]
    inner = layers - RADIUS
    odd = lax.axis_index("dom") & 1
    one, two = -0.5 / HALF_WIDTH, -1.0 / HALF_WIDTH

    @pl.when(odd == 0)
    def _():
        add_above(got, v.at[:, :RADIUS], halo, one)
        add_below(part.at[:, :RADIUS], halo, edge, two)

    @pl.when(odd == 1)
    def _():
        add_below(got, v.at[:, inner:], halo, one)
        add_above(part.at[:, inner:], halo, edge, two)

    block[...] = as_halves(edge[...])
    deal(block, chunks)


def split_3(values):
    high = values.astype(jnp.bfloat16)
    rest = values - high.astype(jnp.float32)
    middle = rest.astype(jnp.bfloat16)
    low = (rest - middle.astype(jnp.float32)).astype(jnp.bfloat16)
    return jnp.concatenate([high, middle, low], axis=0)


def lane_block(lane):
    block = lane >> 4
    first = jnp.where(block < 3, 0, jnp.where(block < 5, 1, 2))
    second = jnp.where(block < 3, block + 1, jnp.where(block < 5, block - 1, 3))
    return block, 4 * first + ((lane >> 2) & 3), 4 * second + (lane & 3)


def row_products(loads, rows, left_rows, right_rows):
    left, right = [], []
    for load in loads:
        high, low = split(load().reshape(rows, 128))
        left += [high, high, low]
        right += [high, low, high]
    total = lax.dot_general(
        jnp.concatenate(left, axis=1)[left_rows],
        jnp.concatenate(right, axis=1)[right_rows],
        NT,
        preferred_element_type=jnp.float32,
    )
    row = lax.broadcasted_iota(jnp.int32, total.shape, 0)
    column = lax.broadcasted_iota(jnp.int32, total.shape, 1)
    total = jnp.where((row & 7) == (column & 7), total, 0.0)
    return jnp.sum(total.reshape(total.shape[0] // 8, 8, total.shape[1]), axis=1)


def pack(sums, column_orbital, row_orbital):
    count, columns = sums.shape
    lane = lax.broadcasted_iota(jnp.int32, (columns, 128), 1)
    orbital = lax.broadcasted_iota(jnp.int32, (columns, 128), 0) >> 3
    wide = jnp.dot(
        split_3(sums),
        place(orbital == column_orbital(lane)),
        preferred_element_type=jnp.float32,
    )
    wide = wide[:count] + wide[count : 2 * count] + wide[2 * count :]
    lane = lax.broadcasted_iota(jnp.int32, (count, 128), 1)
    orbital = lax.broadcasted_iota(jnp.int32, (count, 128), 0)
    return jnp.sum(jnp.where(orbital == row_orbital(lane), wide, 0.0), axis=0, keepdims=True)


def own_gram(early, near, far, out, own):
    orbs, layers = out.shape[0], out.shape[1]
    first, _ = far_near_starts(layers)
    rest = RADIUS - (first * RADIUS) // (layers - RADIUS)
    out[:, pl.ds(first, RADIUS)] = far[...].reshape(orbs, RADIUS, 16, 128)
    out[:, pl.ds(rest, layers - RADIUS)] = near[...].reshape(orbs, layers - RADIUS, 16, 128)
    everything = slice(None)
    loads = [lambda h=h: near[:, h] for h in range(near.shape[1])]
    loads += [lambda h=h: far[:, h] for h in range(far.shape[1])]
    sums = row_products(loads, 8 * orbs, everything, everything)
    sums = jnp.concatenate([sums, jnp.zeros_like(sums)], axis=0)
    lanes = pack(sums, lambda lane: lane & 3, lambda lane: (lane >> 2) & 3)
    lane = lax.broadcasted_iota(jnp.int32, (1, 128), 1)
    own[...] = early[...] + jnp.where((lane >= 96) & (lane < 112), lanes, 0.0)


def gram_lanes(chunks, rows):
    orbs, depth = chunks[0].shape[0], chunks[0].shape[1]
    me = lax.axis_index("orb")
    for k, chunk in enumerate(chunks):
        first = (me ^ k) * orbs
        for o in range(orbs):
            for h in range(depth):
                rows[h, first + o] = chunk[o, h]
    loads = [lambda h=h: rows[h] for h in range(depth)]
    sums = row_products(loads, 128, slice(0, 96), slice(32, 128))
    sums = jnp.concatenate([sums, jnp.zeros((4, 96), jnp.float32)], axis=0)
    lanes = pack(sums, lambda lane: lane_block(lane)[2] - 4, lambda lane: lane_block(lane)[1])
    lane = lax.broadcasted_iota(jnp.int32, (1, 128), 1)
    return jnp.where(lane < 96, lanes, 0.0)


def near_gram(got_2, got_3, got_1, own, out, rows):
    out[...] = gram_lanes((own, got_1, got_2, got_3), rows)


def far_gram(others, got_2, got_3, got_1, own, out, rows):
    lanes = gram_lanes((own, got_1, got_2, got_3), rows) + others[...]
    out[...] = jnp.broadcast_to(lanes[None], out.shape)


def final_kernel(cells, terms, out):
    orbs = 4
    sums = [terms[q] for q in range(orbs)]
    for d in range(1, terms.shape[0] // orbs):
        for q in range(orbs):
            sums[q] = sums[q] + terms[d * orbs + q]
    across = sums[0] + sums[1] + sums[2] + sums[3]
    row = lax.broadcasted_iota(jnp.int32, (16, 128), 0)
    lane = lax.broadcasted_iota(jnp.int32, (16, 128), 1)
    block, first, second = lane_block(lane)
    own = jnp.where(
        row < 8,
        jnp.where(row < 4, sums[0], sums[1]),
        jnp.where(row < 12, sums[2], sums[3]),
    )
    upper = jnp.where((block < 6) & (first == row), across, 0.0)
    lower = jnp.where((block < 6) & (second == row), across, 0.0)
    own = jnp.where((block == 6) & (((lane >> 2) & 3) == (row & 3)), own, 0.0)
    column = lax.broadcasted_iota(jnp.int32, (128, 16), 1)
    lane = lax.broadcasted_iota(jnp.int32, (128, 16), 0)
    block, first, second = lane_block(lane)

    def unpack(values, condition):
        parts = jnp.dot(split_3(values), place(condition), preferred_element_type=jnp.float32)
        return parts[:16] + parts[16:32] + parts[32:]

    total = unpack(upper, second == column) + unpack(lower, first == column)
    same = (lax.broadcasted_iota(jnp.int32, (16, 16), 0) >> 2) == (
        lax.broadcasted_iota(jnp.int32, (16, 16), 1) >> 2
    )
    total = total + jnp.where(same, unpack(own, (lane & 3) == (column & 3)), 0.0)
    out[...] = total * (1.0 / cells)


def call(kernel, outs, in_specs, scratch=(), flops=10_000_000, limit=48 * 2**20):
    return pl.pallas_call(
        kernel,
        out_shape=outs,
        in_specs=in_specs,
        out_specs=jax.tree.map(lambda _: pl.BlockSpec(memory_space=VMEM), outs),
        scratch_shapes=list(scratch),
        compiler_params=pltpu.CompilerParams(vmem_limit_bytes=limit),
        cost_estimate=pl.CostEstimate(flops=flops, bytes_accessed=2**21, transcendentals=0),
    )


def on_device(
    orbitals, local_potential, sphere_index, projector, species, atom_count, channel_energy
):
    f32 = jnp.float32
    in_vmem = pl.BlockSpec(memory_space=VMEM)
    orbs, layers, wide, deep = orbitals.shape
    doms, orb_devices = lax.axis_size("dom"), lax.axis_size("orb")
    far_pairs = [(i, (i - 1 if i % 2 == 0 else i + 1) % doms) for i in range(doms)]
    near_pairs = [(i, i ^ 1) for i in range(doms)]
    edge = jax.ShapeDtypeStruct((orbs, RADIUS, wide, deep), f32)
    block = jax.ShapeDtypeStruct(orbitals.shape, f32)
    atoms, points = sphere_index.shape
    scalars = (species, atom_count, channel_energy)
    fields = (orbitals, local_potential, sphere_index, projector)
    far, near = call(order_edges, (edge, edge), [in_vmem] * 2)(
        orbitals[:, :RADIUS], orbitals[:, layers - RADIUS :]
    )
    got_far = lax.ppermute(far, "dom", far_pairs)
    got_near = lax.ppermute(near, "dom", near_pairs)
    scratch = [
        pltpu.VMEM((2, orbs * deep, layers * wide), jnp.bfloat16),
        pltpu.VMEM((orbs,) + sphere_index.shape, f32),
        pltpu.VMEM((2, orbs * deep, atoms * points), jnp.bfloat16),
    ]
    far, near, part, rowhot, zhot, strength = call(
        first_kernel,
        (
            edge,
            edge,
            block,
            jax.ShapeDtypeStruct((layers * wide, atoms * points), jnp.bfloat16),
            jax.ShapeDtypeStruct((deep, atoms * points), jnp.bfloat16),
            jax.ShapeDtypeStruct((projector.shape[1], atoms, deep), f32),
        ),
        [in_vmem] * 7,
        scratch,
        flops=3_000_000_000,
    )(*scalars, *fields)
    next_far = lax.ppermute(far, "dom", far_pairs)
    next_near = lax.ppermute(near, "dom", near_pairs)
    part = call(
        second_kernel,
        block,
        [in_vmem] * 10,
        scratch + [pltpu.VMEM(orbitals.shape, f32)],
        flops=3_000_000_000,
    )(*fields, strength, rowhot, zhot, got_near, got_far, part)

    def halves(count):
        return jax.ShapeDtypeStruct((orbs, 2 * count, wide // 2, deep), f32)

    def swap(chunks):
        return {
            k: lax.ppermute(chunks[k], "orb", [(i, i ^ k) for i in range(orb_devices)])
            for k in (2, 3, 1)
        }

    def rows_of(chunk):
        return [pltpu.VMEM((chunk.shape[1], orbs * orb_devices) + chunk.shape[2:], f32)]

    def chunk(count):
        return jax.ShapeDtypeStruct((orbs, 2 * count // orb_devices, wide // 2, deep), f32)

    row = jax.ShapeDtypeStruct((1, 128), f32)
    inner = layers - RADIUS
    edges = [pltpu.VMEM(edge.shape, f32)] * 2
    near, *sends = call(
        second_near, (halves(inner),) + (chunk(inner),) * 4, [in_vmem] * 3, edges
    )(part, orbitals, next_near)
    own_near, got_early = sends[0], swap(sends)
    far, *sends = call(
        second_far, (halves(RADIUS),) + (chunk(RADIUS),) * 4, [in_vmem] * 3, edges
    )(part, orbitals, next_far)
    own_far, got_late = sends[0], swap(sends)
    early = call(near_gram, row, [in_vmem] * 4, rows_of(own_near), flops=1_000_000_000)(
        got_early[2], got_early[3], got_early[1], own_near
    )
    filtered, others = call(own_gram, (block, row), [in_vmem] * 3, flops=1_500_000_000)(
        early, near, far
    )
    terms = call(
        far_gram,
        jax.ShapeDtypeStruct((doms * orb_devices, 1, 128), f32),
        [in_vmem] * 5,
        rows_of(own_far),
    )(others, got_late[2], got_late[3], got_late[1], own_far)
    terms = lax.all_to_all(terms, ("dom", "orb"), 0, 0)
    gram = call(
        functools.partial(final_kernel, float(layers * wide * deep * doms)),
        jax.ShapeDtypeStruct((16, 16), f32),
        [in_vmem],
    )(terms)
    return filtered, gram


def solution(mesh):
    placed = (
        P("orb", "dom", None, None),
        P("dom", None, None),
        P("dom", None),
        P("dom", None, None),
        P("dom"),
        P("dom"),
        P(),
    )
    return jax.shard_map(
        on_device,
        mesh=mesh,
        in_specs=placed,
        out_specs=(P("orb", "dom", None, None), P()),
        check_vma=False,
    )
```
